32 devices in a mesh: expert: 8 (over z, x), tensor: 4 (over y, core).
Axes of the slice: x: 2, y: 2, z: 4, core: 2. Of those that a mesh axis runs over, the one named last changes fastest.
Arguments:
- tokens: bfloat16 [4096, 768], P('expert'), may hold values from -6 to 6
- doc_lengths: int32 [8, 4], P('expert'), may hold values from 1 to 256, 512 in all within a row
- routes: int32 [4096, 1], P('expert'), may hold values from 0 to 7; in each aligned block of 512 rows (0 to 511, 512 to 1023, ...) at most 128 rows name the same one
- gain_first: float32 [768], replicated, may hold values from 0.5 to 1.5
- projections: bfloat16 [3, 768, 768], P(None, None, 'tensor'), may hold values from -0.21875 to 0.21875
- attention_out: bfloat16 [768, 768], P('tensor'), may hold values from -1.75 to 1.75
- relative_bias_table: float32 [32, 12], P(None, 'tensor'), may hold values from -4 to 4
- gain_second: float32 [768], replicated, may hold values from 0.5 to 1.5
- router_weight: bfloat16 [768, 8], replicated, may hold values from -0.15625 to 0.15625
- expert_in: bfloat16 [8, 768, 3072], P('expert', None, 'tensor'), may hold values from -0.21875 to 0.21875
- expert_out: bfloat16 [8, 3072, 768], P('expert', 'tensor'), may hold values from -2 to 2
- cotangent: bfloat16 [4096, 768], P('expert'), may hold values from -6 to 6
Outputs:
- layer_output: bfloat16 [4096, 768], P('expert')
- grad_tokens: float32 [4096, 768], P('expert')
- grad_gain_first: float32 [768], replicated
- grad_projections: float32 [3, 768, 768], P(None, None, 'tensor')
- grad_attention_out: float32 [768, 768], P('tensor')
- grad_position_table: float32 [32, 12], P(None, 'tensor')
- grad_gain_second: float32 [768], replicated
- grad_router: float32 [768, 8], replicated
- grad_expert_in: float32 [8, 768, 3072], P('expert', None, 'tensor')
- grad_expert_out: float32 [8, 3072, 768], P('expert', 'tensor')
The draws below stay inside these ranges and needn't reach their ends.
Inputs may be any that keep to these rules, and one draw needn't show every extreme that they name: `doc_lengths`: each row sums to 512; its longest entry is exactly 256. `routes`: among the 512 rows of one token group no expert is named more than 128 times; in some group one expert is named exactly 128 times; every expert is named somewhere.
All inputs are finite; a program needn't handle non-finite values.
Results may differ from the reference program's by a relative error of at most 0.013.
The reference program's roundings to bfloat16 on the way count: a program that leaves them out, or rounds other values in their place, can miss the bound.
Values may be sent and summed in bfloat16 or wider, within the bound.
A program may use at most 128 MiB of HBM per device.

```python
import math
import jax
import jax.numpy as jnp
import numpy as np
from jax import lax

D = 768
HEADS = 12
HD = 64
FF = 3072
BUCKETS = 32
GROUP_TOKENS = 512
SEQS = 4
EXPERTS = 8
GROUPS = 8
TOKENS = 4096
MOST_LEN = 256
CAP = 128


def block_levels(rng, shape, shards, least, top_value):
    loudness = 1.0
    for position, parts in shards:
        steps = jax.random.uniform(jax.random.fold_in(jax.random.fold_in(rng, 6), position), (parts,), jnp.float32, least / len(shards), top_value / len(shards))
        loudness = loudness * jnp.repeat(jnp.exp(steps), shape[position] // parts).reshape((-1,) + (1,) * (len(shape) - 1 - position))
    return loudness


def length_profile(count, total, limit, slope):
    portions = [(1 << 20) // math.isqrt(standing ** slope) + 1 for standing in range(2, count + 1)]
    surplus, given = total - limit - (count - 1), [1] * (count - 1)
    while surplus > 0:
        candidates = [i for i in range(count - 1) if given[i] < limit]
        whole, left = sum([portions[i] for i in candidates]), surplus
        for i in candidates:
            more = min(limit - given[i], max(1, left * portions[i] // whole), surplus)
            given[i] = given[i] + more
            surplus = surplus - more
    return np.array([limit] + given)


def uneven(rng, amount, total, most, skew):
    if amount == 2:
        one = jax.random.randint(rng, (), max(1, total - most), min(most, total - 1) + 1)
        return jnp.stack([one, total - one])
    sizes = jnp.asarray(length_profile(amount, total, most, skew), jnp.int32)
    pairs = (amount - 1) // 2
    donor, sink = sizes[1:1 + 2 * pairs:2], sizes[2:2 + 2 * pairs:2]
    slack = jnp.minimum(donor - 1, most - sink)
    moved = jax.random.randint(jax.random.fold_in(rng, 1), (pairs,), 0, 1 << 20) % (slack + 1)
    sizes = sizes.at[1:1 + 2 * pairs:2].set(donor - moved).at[2:2 + 2 * pairs:2].set(sink + moved)
    return sizes[jax.random.permutation(jax.random.fold_in(rng, 2), amount)]


def deal_out(key, own, number, rows, count, top, most, skew):
    sequence = jax.random.permutation(key, count)
    packed, usual = portions_of(count, rows * top, most, skew, True), portions_of(count, rows * top, most, skew, False)
    places = jnp.arange(count)

    def named(sizes, turn):
        used = int((sizes > 0).sum())
        fixed = max(1, used // 4)
        moved = fixed + (places - fixed + turn * (used - fixed)) % max(1, count - fixed)
        return jnp.zeros((count,), jnp.int32).at[sequence[jnp.where(places < fixed, places, moved)]].set(jnp.asarray(sizes, jnp.int32))

    sizes = jnp.where(number % 4 == 0, named(packed, number // 4), named(usual, number - number // 4 - 1))
    mixed = jax.random.permutation(jax.random.fold_in(own, 3), count)
    donor, receiver = mixed[0:count // 2 * 2:2], mixed[1:count // 2 * 2:2]
    margin = jnp.minimum(sizes[donor] - 1, most - sizes[receiver]) // 2
    margin = jnp.where((donor == sequence[0]) | (receiver == sequence[0]) | (sizes[receiver] == 0), 0, jnp.maximum(margin, 0))
    moved = jax.random.randint(jax.random.fold_in(own, 4), (count // 2,), 0, 1 << 20) % (margin + 1)
    sizes = sizes.at[donor].add(-moved).at[receiver].add(moved)
    members = jnp.searchsorted(jnp.cumsum(sizes), jnp.arange(rows * top), side="right").astype(jnp.int32)
    listing = members.reshape(top, rows).T
    listing = listing[jax.random.permutation(jax.random.fold_in(own, 1), rows)]
    turn = jax.random.randint(jax.random.fold_in(own, 2), (rows, 1), 0, top)
    return jnp.take_along_axis(listing, (jnp.arange(top)[None, :] + turn) % top, axis=1)


def portions_of(count, total, most, lean, full):
    weights = [(1 << 20) // math.isqrt(rank ** lean) + 1 for rank in range(1, count + 1)]
    largest = most if full else min(most, max(-(-total // count), total * weights[0] // sum(weights)))
    least = 1 if total - largest >= count - 1 else 0
    counts, rest = [largest] + [least] * (count - 1), total - largest - least * (count - 1)
    while rest > 0:
        candidates = [i for i in range(1, count) if counts[i] < largest] or [i for i in range(1, count) if counts[i] < most]
        mass, budget = sum([weights[i] for i in candidates]), rest
        for i in candidates:
            addition = min(most - counts[i], max(1, budget * weights[i] // mass), rest)
            counts[i] = counts[i] + addition
            rest = rest - addition
    return np.array(counts)


def normal_values(stream_key, extent, spread, reach, pieces=(), kind=jnp.bfloat16):
    loudness = block_levels(stream_key, extent, pieces, -0.22, 0.18) if pieces else 1.0
    drawn = jax.random.normal(stream_key, extent, jnp.float32) * spread * loudness
    return jnp.minimum(jnp.maximum(drawn, -reach), reach).astype(kind)


def setup_inputs(seed: int = 0) -> dict:
    seeds = jax.random.split(jax.random.key(seed), 13)
    tokens = normal_values(seeds[0], (TOKENS, D), 1.0, 6.0, ((0, 8),))
    doc_lengths = jax.vmap(lambda own: uneven(own, SEQS, GROUP_TOKENS, MOST_LEN, 2))(jax.random.split(seeds[1], GROUPS)).reshape((GROUPS, SEQS)).astype(jnp.int32)
    routes_keys = jax.random.split(jax.random.fold_in(seeds[2], 1), TOKENS // GROUP_TOKENS)
    routes_turns = jax.random.permutation(jax.random.fold_in(seeds[2], 3), TOKENS // GROUP_TOKENS)
    routes = jax.vmap(lambda own, number: deal_out(jax.random.fold_in(seeds[2], 2), own, number, GROUP_TOKENS, EXPERTS, 1, CAP, 1))(routes_keys, routes_turns).reshape((TOKENS, 1))
    gain_first = jnp.clip(1.0 + 0.1 * jax.random.normal(seeds[3], (D,), jnp.float32), 0.5, 1.5)
    projections = normal_values(seeds[4], (3, D, HEADS * HD), D ** -0.5, 0.21875, ((2, 4),))
    attention_out = normal_values(seeds[5], (HEADS * HD, D), (HEADS * HD // 64) ** -0.5, 1.75, ((0, 4),))
    relative_bias_table = normal_values(seeds[6], (BUCKETS, HEADS), 1.0, 4.0, ((1, 4),), jnp.float32)
    gain_second = jnp.clip(1.0 + 0.1 * jax.random.normal(seeds[7], (D,), jnp.float32), 0.5, 1.5)
    router_weight = normal_values(seeds[8], (D, EXPERTS), (2 * D) ** -0.5, 0.15625)
    expert_in = normal_values(seeds[9], (EXPERTS, D, FF), D ** -0.5, 0.21875, ((0, 8), (2, 4)))
    expert_out = normal_values(seeds[10], (EXPERTS, FF, D), (EXPERTS * 0.018 * ((3072 // FF) // 8 + 1)), 2.0, ((0, 8), (1, 4)))
    cotangent = normal_values(seeds[11], (TOKENS, D), 1.0, 6.0, ((0, 8),))
    return {"tokens": tokens, "doc_lengths": doc_lengths, "routes": routes, "gain_first": gain_first, "projections": projections, "attention_out": attention_out, "relative_bias_table": relative_bias_table, "gain_second": gain_second, "router_weight": router_weight, "expert_in": expert_in, "expert_out": expert_out, "cotangent": cotangent}


@jax.custom_vjp
def low(v):
    return lax.optimization_barrier(v.astype(jnp.bfloat16)).astype(jnp.float32)

@jax.custom_vjp
def low_back(v):
    return v

def low_keep(v):
    return (low(v), None)

def low_pass(kept, grad):
    return (grad,)

def back_keep(v):
    return (v, None)

def back_low(kept, grad):
    return (low(grad),)
low.defvjp(low_keep, low_pass)
low_back.defvjp(back_keep, back_low)
edge_list = (1, 2, 3, 4, 5, 6, 7, 8, 12, 16, 23, 32, 46, 64, 91)
tiny_eps = 1e-06
masked_score = -1e+30
largest_logit = lax.Precision.HIGHEST

def bucket_table(row_count):
    places = jnp.arange(row_count, dtype=jnp.int32)
    offsets = places[:, None] - places[None, :]
    distance = jnp.abs(offsets)
    bounds = jnp.asarray(edge_list, dtype=jnp.int32)
    passed = lax.optimization_barrier(jnp.sum((distance[:, :, None] >= bounds[None, None, :]).astype(jnp.int32), axis=2)).astype(jnp.int32)
    return passed + 16 * (offsets < 0).astype(jnp.int32)

def document_mask(lengths_row, row_count):
    places = jnp.arange(row_count, dtype=jnp.int32)
    endings = jnp.cumsum(lengths_row.astype(jnp.int32)).astype(jnp.int32)
    document = lax.optimization_barrier(jnp.sum((places[:, None] >= endings[None, :]).astype(jnp.int32), axis=1)).astype(jnp.int32)
    return document[:, None] == document[None, :]

def rms_scale(values, gain):
    return values * lax.rsqrt(lax.optimization_barrier(jnp.mean(values * values, axis=-1, keepdims=True)) + tiny_eps) * gain

def gelu_curve(values):
    return 0.5 * values * (1.0 + jnp.tanh(0.7978845608 * (values + 0.044715 * values * values * values)))

def softmax_rows(scores):
    top_score = lax.optimization_barrier(jnp.max(scores, axis=-1, keepdims=True))
    raised = jnp.exp(scores - top_score)
    return raised / lax.optimization_barrier(jnp.sum(raised, axis=-1, keepdims=True))

def group_mask(lengths_row):
    return document_mask(lengths_row, GROUP_TOKENS)

def reference(tokens, doc_lengths, routes, gain_first, projections, attention_out, relative_bias_table, gain_second, router_weight, expert_in, expert_out, cotangent):
    route_column = routes[:, 0].astype(jnp.int32)
    chosen = route_column[:, None] == jnp.arange(EXPERTS, dtype=jnp.int32)[None, :]
    earlier = jnp.cumsum(chosen.astype(jnp.int32).reshape(GROUPS, GROUP_TOKENS, EXPERTS), axis=1).astype(jnp.int32).reshape(TOKENS, EXPERTS) - 1
    capacity_position = lax.optimization_barrier(jnp.sum(jnp.where(chosen, earlier, 0), axis=1)).astype(jnp.int32)
    row_index = jnp.arange(TOKENS, dtype=jnp.int32) // GROUP_TOKENS * CAP + capacity_position
    bucket_ids = bucket_table(GROUP_TOKENS)
    allowed = jax.vmap(group_mask)(doc_lengths)
    score_scale = HD ** (-0.5)

    def forward(token_float, first_gain, proj_weight, out_weight, table, second_gain, router_float, first_weights, second_weights):
        normed_first = low(rms_scale(token_float, first_gain))

        def attend(pack):
            rows, mask_here = pack
            projected = low(low_back(jnp.einsum('nd,cdh->cnh', rows, proj_weight, precision=largest_logit)))
            queries = projected[0].reshape(GROUP_TOKENS, HEADS, HD)
            keys_here = projected[1].reshape(GROUP_TOKENS, HEADS, HD)
            values_here = projected[2].reshape(GROUP_TOKENS, HEADS, HD)
            position_bias = jnp.transpose(table[bucket_ids], (2, 0, 1))
            scores = low_back(jnp.einsum('qhd,khd->hqk', queries, keys_here, precision=largest_logit) * score_scale + position_bias)
            scores = jnp.where(mask_here[None], scores, masked_score)
            soft_weights = softmax_rows(scores)
            mixed_heads = jnp.einsum('hqk,khd->qhd', low(soft_weights), values_here, precision=largest_logit).reshape(GROUP_TOKENS, HEADS * HD)
            mixed_heads = low(low_back(mixed_heads))
            return low_back(jnp.dot(mixed_heads, out_weight, precision=largest_logit))
        attended = lax.map(jax.checkpoint(attend), (normed_first.reshape(GROUPS, GROUP_TOKENS, D), allowed)).reshape(TOKENS, D)
        after_attention = token_float + attended
        normed_second = low(rms_scale(after_attention, second_gain))
        router_probs = softmax_rows(jnp.dot(normed_second, router_float, precision=largest_logit))
        gate_value = lax.optimization_barrier(jnp.sum(jnp.where(chosen, router_probs, 0.0), axis=1))
        send_rows = low_back(normed_second)
        buffer = jnp.zeros((EXPERTS, GROUPS * CAP, D), jnp.float32).at[route_column, row_index].set(send_rows)

        def expert(pack):
            rows, first_weight, second_weight = pack
            pre_active = low_back(jnp.dot(rows, first_weight, precision=largest_logit))
            hidden_units = low(gelu_curve(pre_active))
            return low(low_back(jnp.dot(hidden_units, second_weight, precision=largest_logit)))
        expert_rows = lax.map(jax.checkpoint(expert), (buffer, first_weights, second_weights))
        picked = expert_rows[route_column, row_index]
        return after_attention + gate_value[:, None] * picked
    result, pullback = jax.vjp(forward, tokens.astype(jnp.float32), gain_first, projections.astype(jnp.float32), attention_out.astype(jnp.float32), relative_bias_table, gain_second, router_weight.astype(jnp.float32), expert_in.astype(jnp.float32), expert_out.astype(jnp.float32))
    grads = pullback(cotangent.astype(jnp.float32))
    return (result.astype(jnp.bfloat16), grads[0], grads[1], grads[2], grads[3], grads[4], grads[5], grads[6], grads[7], grads[8])
```

```python
import functools

import jax
import jax.numpy as jnp
from jax import lax
from jax.experimental import pallas as pl
from jax.experimental.pallas import tpu as pltpu
from jax.sharding import PartitionSpec as P

edge_list = (1, 2, 3, 4, 5, 6, 7, 8, 12, 16, 23, 32, 46, 64, 91)
tiny_eps = 1e-06
masked_score = -1e30
largest_logit = lax.Precision.HIGHEST


def offset_buckets(row_count):
    span = 2 * row_count
    places = jnp.arange(span, dtype=jnp.int32)
    offsets = jnp.where(places < row_count, -places, span - places)
    bounds = jnp.asarray(edge_list, dtype=jnp.int32)
    passed = jnp.sum((jnp.abs(offsets)[:, None] >= bounds[None, :]).astype(jnp.int32), axis=1)
    return passed + 16 * (offsets < 0).astype(jnp.int32)


def document_ids(lengths_row, row_count):
    places = jnp.arange(row_count, dtype=jnp.int32)
    endings = jnp.cumsum(lengths_row)
    return jnp.sum((places[:, None] >= endings[None, :]).astype(jnp.int32), axis=1)


def rms_scale(values, gain):
    return values * lax.rsqrt(jnp.mean(values * values, axis=-1, keepdims=True) + tiny_eps) * gain


def gelu_curve(values):
    return (
        0.5
        * values
        * (1.0 + jnp.tanh(0.7978845608 * (values + 0.044715 * values * values * values)))
    )


def softmax_rows(scores):
    top_score = jnp.max(scores, axis=-1, keepdims=True)
    raised = jnp.exp(scores - top_score)
    return raised / jnp.sum(raised, axis=-1, keepdims=True)


MESH = pl.DeviceIdType.MESH


def vmem():
    return pl.BlockSpec(memory_space=pltpu.VMEM)


def tensor_places():
    mine = lax.axis_index("tensor")
    core = mine % 2
    side = mine // 2
    return mine, core, side, side * 2 + (1 - core), (1 - side) * 2 + core


def greet(devices):
    barrier = pltpu.get_barrier_semaphore()
    for device in devices:
        pl.semaphore_signal(barrier, inc=1, device_id=device, device_id_type=MESH)
    pl.semaphore_wait(barrier, len(devices))


def remote(source, target, send_sem, recv_sem, device):
    return pltpu.make_async_remote_copy(
        src_ref=source,
        dst_ref=target,
        send_sem=send_sem,
        recv_sem=recv_sem,
        device_id=device,
        device_id_type=MESH,
    )


def tensor_sum_kernel(x_ref, o_ref, near, chip, far, send_sem, recv_sem):
    _, core, _, sibling, across = tensor_places()
    half = x_ref.shape[0] // 2
    greet([{"tensor": sibling}, {"tensor": across}])
    own = pl.ds(pl.multiple_of(core * half, half), half)
    other = pl.ds(pl.multiple_of((1 - core) * half, half), half)
    first = remote(x_ref.at[other], near, send_sem.at[0], recv_sem.at[0], {"tensor": sibling})
    first.start()
    first.wait()
    chip[...] = (x_ref[own].astype(jnp.float32) + near[...].astype(jnp.float32)).astype(chip.dtype)
    second = remote(chip, far, send_sem.at[1], recv_sem.at[1], {"tensor": across})
    second.start()
    second.wait()
    o_ref[own] = chip[...].astype(jnp.float32) + far[...].astype(jnp.float32)
    third = remote(
        o_ref.at[own], o_ref.at[own], send_sem.at[2], recv_sem.at[2], {"tensor": sibling}
    )
    third.start()
    third.wait()


def tensor_total(value, collective_id):
    rows, width = value.shape
    if lax.axis_size("tensor") != 4 or rows % 32:
        return lax.psum(value, "tensor")
    half = pltpu.VMEM((rows // 2, width), jnp.bfloat16)
    return pl.pallas_call(
        tensor_sum_kernel,
        out_shape=jax.ShapeDtypeStruct((rows, width), jnp.float32),
        in_specs=[vmem()],
        out_specs=vmem(),
        scratch_shapes=[
            half,
            half,
            half,
            pltpu.SemaphoreType.DMA((3,)),
            pltpu.SemaphoreType.DMA((3,)),
        ],
        compiler_params=pltpu.CompilerParams(
            collective_id=collective_id, has_side_effects=True, vmem_limit_bytes=32 * 2**20
        ),
        cost_estimate=pl.CostEstimate(flops=0, bytes_accessed=30_000_000, transcendentals=0),
    )(value.astype(jnp.bfloat16))


def share_over_tensor(places, pieces, sems):
    mine, _, _, sibling, across = places
    across_send, across_recv, near_send, near_recv, pass_send, pass_recv = sems

    def begin(step):
        far = remote(
            pieces(mine, step),
            pieces(mine, step),
            across_send.at[step],
            across_recv.at[step],
            {"tensor": across},
        )
        close = remote(
            pieces(mine, step),
            pieces(mine, step),
            near_send.at[step],
            near_recv.at[step],
            {"tensor": sibling},
        )
        far.start()
        close.start()
        return far, close

    def forward(step):
        onward = remote(
            pieces(across, step),
            pieces(across, step),
            pass_send.at[step],
            pass_recv.at[step],
            {"tensor": sibling},
        )
        onward.start()
        return onward

    return begin, forward


def dispatch_kernel(groups, send_ref, o_ref, out_send, out_recv, *sems):
    here = lax.axis_index("expert")
    places = tensor_places()
    mine, _, _, sibling, across = places
    peers = [lax.rem(here + step, groups) for step in range(groups)]
    greet([{"expert": peer} for peer in peers[1:]] + [{"tensor": sibling}, {"tensor": across}])
    copies = [None]
    for step in range(1, groups):
        copy = remote(
            send_ref.at[peers[step]],
            o_ref.at[mine, here],
            out_send.at[step],
            out_recv.at[step],
            {"expert": peers[step]},
        )
        copy.start()
        copies.append(copy)
    o_ref[mine, here] = send_ref[here]

    def pieces(quarter, step):
        return o_ref.at[quarter, lax.rem(here + groups - step, groups)]

    begin, forward = share_over_tensor(places, pieces, sems)
    shared = []
    for step in range(groups):
        if step:
            copies[step].wait_recv()
        shared.append(begin(step))
    onward = []
    for step in range(groups):
        shared[step][0].wait_recv()
        onward.append(forward(step))
    for step in range(groups):
        if step:
            copies[step].wait_send()
        shared[step][0].wait_send()
        shared[step][1].wait()
        onward[step].wait()


def kernels_fit(part_rows):
    return lax.axis_size("tensor") == 4 and lax.axis_size("expert") <= 8 and part_rows % 16 == 0


def dispatch(send, collective_id):
    groups, part, width = send.shape
    if collective_id is None or not kernels_fit(part):
        received = lax.all_to_all(send, "expert", split_axis=0, concat_axis=0, tiled=True)
        return lax.all_gather(received, "tensor", axis=0, tiled=False)
    sems = pltpu.SemaphoreType.DMA((groups,))
    return pl.pallas_call(
        functools.partial(dispatch_kernel, groups),
        out_shape=jax.ShapeDtypeStruct((lax.axis_size("tensor"),) + send.shape, send.dtype),
        in_specs=[vmem()],
        out_specs=vmem(),
        scratch_shapes=[sems] * 8,
        compiler_params=pltpu.CompilerParams(
            collective_id=collective_id, has_side_effects=True, vmem_limit_bytes=32 * 2**20
        ),
        cost_estimate=pl.CostEstimate(flops=0, bytes_accessed=50_000_000, transcendentals=0),
    )(send)


def combine_kernel(groups, ahead_ref, back_ref, o_ref, near, chip, far, total, *sems):
    near_send, near_recv, far_send, far_recv, out_send, out_recv = sems[:6]
    here = lax.axis_index("expert")
    places = tensor_places()
    mine, core, side, sibling, across = places
    peers = [lax.rem(here + step, groups) for step in range(groups)]
    greet([{"expert": peer} for peer in peers[1:]] + [{"tensor": sibling}, {"tensor": across}])
    inputs = (ahead_ref, back_ref)
    sides = (1 - side, side)
    gather = []
    for kind in range(2):
        for turn in range(2):
            copy = remote(
                inputs[kind].at[sides[turn] * 2 + (1 - core)],
                near.at[2 * kind + turn],
                near_send.at[2 * kind + turn],
                near_recv.at[2 * kind + turn],
                {"tensor": sibling},
            )
            copy.start()
            gather.append(copy)
    crossing = []
    for kind in range(2):
        for turn in range(2):
            gather[2 * kind + turn].wait_recv()
            chip[2 * kind + turn] = (
                inputs[kind][sides[turn] * 2 + core].astype(jnp.float32)
                + near[2 * kind + turn].astype(jnp.float32)
            ).astype(chip.dtype)
            if turn == 0:
                copy = remote(
                    chip.at[2 * kind],
                    far.at[kind],
                    far_send.at[kind],
                    far_recv.at[kind],
                    {"tensor": across},
                )
                copy.start()
                crossing.append(copy)
    outgoing = []
    for kind in range(2):
        crossing[kind].wait_recv()
        total[kind] = (
            chip[2 * kind + 1].astype(jnp.float32) + far[kind].astype(jnp.float32)
        ).astype(total.dtype)
        outgoing.append(None)
        for step in range(1, groups):
            copy = remote(
                total.at[kind, peers[step]],
                o_ref.at[kind, mine, here],
                out_send.at[kind * groups + step],
                out_recv.at[kind * groups + step],
                {"expert": peers[step]},
            )
            copy.start()
            outgoing.append(copy)
        o_ref[kind, mine, here] = total[kind, here]

    def pieces(quarter, place):
        return o_ref.at[place // groups, quarter, lax.rem(here + groups - place % groups, groups)]

    begin, forward = share_over_tensor(places, pieces, sems[6:])
    shared = []
    for place in range(2 * groups):
        if place % groups:
            outgoing[place].wait_recv()
        shared.append(begin(place))
    onward = []
    for place in range(2 * groups):
        shared[place][0].wait_recv()
        onward.append(forward(place))
    for copy in gather + crossing:
        copy.wait_send()
    for place in range(2 * groups):
        if place % groups:
            outgoing[place].wait_send()
        shared[place][0].wait_send()
        shared[place][1].wait()
        onward[place].wait()


def combine(ahead, back, collective_id):
    quarters, groups, part, width = ahead.shape
    if not kernels_fit(part):
        both = jnp.stack([ahead, back], axis=1).astype(jnp.float32)
        mine = lax.psum_scatter(both, "tensor", scatter_dimension=0, tiled=False)
        received = lax.all_to_all(
            mine.astype(jnp.bfloat16), "expert", split_axis=1, concat_axis=1, tiled=True
        )
        return lax.all_gather(received, "tensor", axis=1, tiled=False)
    piece = (groups, part, width)
    one = pltpu.SemaphoreType.DMA((2 * groups,))
    return pl.pallas_call(
        functools.partial(combine_kernel, groups),
        out_shape=jax.ShapeDtypeStruct((2,) + ahead.shape, jnp.bfloat16),
        in_specs=[vmem(), vmem()],
        out_specs=vmem(),
        scratch_shapes=[
            pltpu.VMEM((4,) + piece, jnp.bfloat16),
            pltpu.VMEM((4,) + piece, jnp.bfloat16),
            pltpu.VMEM((2,) + piece, jnp.bfloat16),
            pltpu.VMEM((2,) + piece, jnp.bfloat16),
            pltpu.SemaphoreType.DMA((4,)),
            pltpu.SemaphoreType.DMA((4,)),
            pltpu.SemaphoreType.DMA((2,)),
            pltpu.SemaphoreType.DMA((2,)),
        ]
        + [one] * 8,
        compiler_params=pltpu.CompilerParams(
            collective_id=collective_id, has_side_effects=True, vmem_limit_bytes=40 * 2**20
        ),
        cost_estimate=pl.CostEstimate(flops=0, bytes_accessed=120_000_000, transcendentals=0),
    )(ahead, back)


def rows_dot(left, right):
    return lax.dot_general(
        left, right, (((1,), (1,)), ((), ())), preferred_element_type=jnp.float32
    )


def columns_dot(left, right):
    return lax.dot_general(
        left, right, (((0,), (0,)), ((), ())), preferred_element_type=jnp.float32
    )


def masked_scores(queries, keys_here, line, doc_column, doc_row, score_scale):
    row_count = queries.shape[0]
    bias = line
    while bias.shape[0] < row_count:
        bias = jnp.concatenate([bias, pltpu.roll(bias, bias.shape[0], 1)], axis=0)
    raw = rows_dot(queries, keys_here) * score_scale + bias[:, :row_count]
    return jnp.where(doc_column == doc_row, raw, masked_score)


def attention_kernel(heads, scale, qkv_ref, line_ref, column_ref, row_ref, mixed_ref, log_ref):
    size = qkv_ref.shape[2] // heads
    for head in range(heads):
        part = slice(head * size, head * size + size)
        scores = masked_scores(
            qkv_ref[0, :, part],
            qkv_ref[1, :, part],
            line_ref[head : head + 1, :],
            column_ref[...],
            row_ref[...],
            scale,
        )
        top_score = jnp.max(scores, axis=-1, keepdims=True)
        raised = jnp.exp(scores - top_score)
        totals = jnp.sum(raised, axis=-1, keepdims=True)
        soft = (raised / totals).astype(jnp.bfloat16)
        mixed_ref[:, part] = jnp.dot(
            soft, qkv_ref[2, :, part], preferred_element_type=jnp.float32
        ).astype(mixed_ref.dtype)
        log_ref[head] = top_score + jnp.log(totals)


def attention_back_kernel(
    heads, scale, qkv_ref, line_ref, column_ref, row_ref, log_ref, up_ref, grad_ref, sums_ref
):
    size = qkv_ref.shape[2] // heads
    row_count = qkv_ref.shape[1]
    for head in range(heads):
        part = slice(head * size, head * size + size)
        queries = qkv_ref[0, :, part]
        keys_here = qkv_ref[1, :, part]
        upstream = up_ref[:, part]
        scores = masked_scores(
            queries,
            keys_here,
            line_ref[head : head + 1, :],
            column_ref[...],
            row_ref[...],
            scale,
        )
        soft = jnp.exp(scores - log_ref[head])
        grad_soft = rows_dot(upstream, qkv_ref[2, :, part])
        centre = jnp.sum(soft * grad_soft, axis=-1, keepdims=True)
        grad_scores = (soft * (grad_soft - centre)).astype(jnp.bfloat16)
        grad_ref[2, :, part] = columns_dot(soft.astype(jnp.bfloat16), upstream).astype(
            grad_ref.dtype
        )
        grad_ref[0, :, part] = (
            jnp.dot(grad_scores, keys_here, preferred_element_type=jnp.float32) * scale
        ).astype(grad_ref.dtype)
        grad_ref[1, :, part] = (columns_dot(grad_scores, queries) * scale).astype(grad_ref.dtype)
        wide = grad_scores.astype(jnp.float32)
        wide = jnp.concatenate([wide, jnp.zeros_like(wide)], axis=1)
        while wide.shape[0] > 1:
            half = wide.shape[0] // 2
            wide = wide[:half] + pltpu.roll(wide[half:], 2 * row_count - half, 1)
        sums_ref[head : head + 1, :] = wide


def local_call(kernel, outs, args):
    return pl.pallas_call(
        kernel,
        out_shape=outs,
        in_specs=[vmem()] * len(args),
        out_specs=tuple(vmem() for _ in outs),
        compiler_params=pltpu.CompilerParams(vmem_limit_bytes=40 * 2**20),
        cost_estimate=pl.CostEstimate(
            flops=1_000_000_000, bytes_accessed=30_000_000, transcendentals=1_000_000
        ),
    )(*args)


def on_device(
    tokens,
    doc_lengths,
    routes,
    gain_first,
    projections,
    attention_out,
    relative_bias_table,
    gain_second,
    router_weight,
    expert_in,
    expert_out,
    cotangent,
):
    row_count = tokens.shape[0]
    model_width = tokens.shape[1]
    heads_here = relative_bias_table.shape[1]
    buckets_total = relative_bias_table.shape[0]
    width_here = projections.shape[2]
    head_size = width_here // heads_here
    experts_total = router_weight.shape[1]
    tensor_size = lax.axis_size("tensor")
    capacity = max(2, 2 * row_count // experts_total)
    part = capacity // tensor_size
    part_rows = experts_total * part
    score_scale = head_size ** (-0.5)
    quarter = lax.axis_index("tensor")

    route_column = routes[:, 0]
    chosen = route_column[:, None] == jnp.arange(experts_total, dtype=jnp.int32)[None, :]
    earlier = jnp.cumsum(chosen.astype(jnp.int32), axis=0) - 1
    slot = jnp.sum(jnp.where(chosen, earlier, 0), axis=1)
    place = (slot // part) * part_rows + route_column * part + slot % part
    own_place = place - quarter * part_rows
    send_pick = (
        jnp.arange(part_rows, dtype=jnp.int32)[:, None] == own_place[None, :]
    ).astype(jnp.bfloat16)
    take_pick = (
        place[:, None] == jnp.arange(tensor_size * part_rows, dtype=jnp.int32)[None, :]
    ).astype(jnp.bfloat16)

    def placed_rows(rows):
        picked_rows = jnp.dot(send_pick, rows, preferred_element_type=jnp.float32)
        return picked_rows.astype(jnp.bfloat16).reshape(experts_total, part, rows.shape[1])

    upstream_rows = dispatch(placed_rows(cotangent), None)

    token_float = tokens.astype(jnp.float32)
    normed_float, first_back = jax.vjp(rms_scale, token_float, gain_first)
    normed_first = normed_float.astype(jnp.bfloat16)
    projected = jnp.einsum(
        "nd,cdh->cnh", normed_first, projections, preferred_element_type=jnp.float32
    ).astype(jnp.bfloat16)
    bucket_pick = (
        jnp.arange(buckets_total, dtype=jnp.int32)[:, None] == offset_buckets(row_count)[None, :]
    ).astype(jnp.float32)
    bias_line = jnp.einsum("bh,bm->hm", relative_bias_table, bucket_pick, precision=largest_logit)
    documents = document_ids(doc_lengths[0], row_count)
    shared_args = (projected, bias_line, documents[:, None], documents[None, :])
    mixed_heads, log_total = local_call(
        functools.partial(attention_kernel, heads_here, score_scale),
        (
            jax.ShapeDtypeStruct((row_count, width_here), jnp.bfloat16),
            jax.ShapeDtypeStruct((heads_here, row_count, 1), jnp.float32),
        ),
        shared_args,
    )
    after_attention = token_float + tensor_total(
        jnp.dot(mixed_heads, attention_out, preferred_element_type=jnp.float32), 0
    )
    second_float, second_back = jax.vjp(rms_scale, after_attention, gain_second)
    normed_second = second_float.astype(jnp.bfloat16)
    normed_wide = normed_second.astype(jnp.float32)
    router_float = router_weight.astype(jnp.float32)
    router_probs = softmax_rows(jnp.dot(normed_wide, router_float, precision=largest_logit))
    gate_value = jnp.sum(jnp.where(chosen, router_probs, 0.0), axis=1)

    gate_high = lax.reduce_precision(gate_value, 8, 7)
    gate_rest = gate_value - gate_high
    gate_middle = lax.reduce_precision(gate_rest, 8, 7)
    gate_terms = jnp.stack([gate_high, gate_middle, gate_rest - gate_middle], axis=1)
    gate_columns = jnp.pad(gate_terms.astype(jnp.bfloat16), ((0, 0), (0, 125)))
    arrived = dispatch(placed_rows(jnp.concatenate([normed_second, gate_columns], axis=1)), 1)
    arrived = arrived.reshape(tensor_size * part_rows, model_width + 128)
    expert_rows = arrived[:, :model_width]
    row_gates = jnp.sum(
        arrived[:, model_width : model_width + 3].astype(jnp.float32), axis=1, keepdims=True
    )
    grad_rows = (
        row_gates * upstream_rows.reshape(expert_rows.shape).astype(jnp.float32)
    ).astype(jnp.bfloat16)
    weight_in = expert_in[0]
    weight_out = expert_out[0]
    pre_active = jnp.dot(expert_rows, weight_in, preferred_element_type=jnp.float32)
    hidden_float, gelu_back = jax.vjp(gelu_curve, pre_active)
    hidden_units = hidden_float.astype(jnp.bfloat16)
    partial_rows = jnp.dot(hidden_units, weight_out, preferred_element_type=jnp.float32)
    grad_hidden = rows_dot(grad_rows, weight_out)
    grad_pre = gelu_back(grad_hidden)[0].astype(jnp.bfloat16)
    grad_inputs = rows_dot(grad_pre, weight_in)
    blocks = (tensor_size, experts_total, part, model_width)
    returned = combine(
        partial_rows.astype(jnp.bfloat16).reshape(blocks),
        grad_inputs.astype(jnp.bfloat16).reshape(blocks),
        2,
    ).reshape(2, tensor_size * part_rows, model_width)
    grad_expert_out = columns_dot(hidden_units, grad_rows)[None]
    grad_expert_in = columns_dot(expert_rows, grad_pre)[None]
    picked = jnp.dot(take_pick, returned[0], preferred_element_type=jnp.float32)
    grad_from_experts = jnp.dot(take_pick, returned[1], preferred_element_type=jnp.float32)
    layer_output = (after_attention + gate_value[:, None] * picked).astype(jnp.bfloat16)
    upstream = cotangent.astype(jnp.float32)
    grad_gate = jnp.sum(upstream * picked, axis=1)
    grad_logits = router_probs * (
        jnp.where(chosen, grad_gate[:, None], 0.0) - (gate_value * grad_gate)[:, None]
    )
    grad_router = jnp.dot(normed_wide.T, grad_logits, precision=largest_logit)
    grad_normed_second = grad_from_experts + jnp.dot(
        grad_logits, router_float.T, precision=largest_logit
    )
    grad_after, grad_gain_second = second_back(grad_normed_second)
    grad_residual = upstream + grad_after
    grad_attention_low = grad_residual.astype(jnp.bfloat16)
    grad_attention_out = columns_dot(mixed_heads, grad_attention_low)
    grad_mixed = rows_dot(grad_attention_low, attention_out).astype(jnp.bfloat16)
    grad_projected, offset_sums = local_call(
        functools.partial(attention_back_kernel, heads_here, score_scale),
        (
            jax.ShapeDtypeStruct((3, row_count, width_here), jnp.bfloat16),
            jax.ShapeDtypeStruct((heads_here, 2 * row_count), jnp.float32),
        ),
        shared_args + (log_total, grad_mixed),
    )
    grad_position_table = jnp.einsum(
        "hm,bm->bh", offset_sums, bucket_pick, precision=largest_logit
    )
    grad_projections = jnp.einsum(
        "nd,cnh->cdh", normed_first, grad_projected, preferred_element_type=jnp.float32
    )
    grad_normed_first = tensor_total(
        jnp.einsum("cnh,cdh->nd", grad_projected, projections, preferred_element_type=jnp.float32),
        3,
    )
    grad_first_in, grad_gain_first = first_back(grad_normed_first)
    grad_tokens = grad_residual + grad_first_in
    large = lax.psum(
        (grad_projections.astype(jnp.bfloat16), grad_attention_out.astype(jnp.bfloat16)), "expert"
    )
    small = lax.psum(
        (grad_position_table, grad_gain_first, grad_gain_second, grad_router), "expert"
    )
    return (
        layer_output,
        grad_tokens,
        small[1],
        large[0].astype(jnp.float32),
        large[1].astype(jnp.float32),
        small[0],
        small[2],
        small[3],
        grad_expert_in,
        grad_expert_out,
    )


def solution(mesh):
    placed = (
        P("expert", None),
        P("expert", None),
        P("expert", None),
        P(),
        P(None, None, "tensor"),
        P("tensor", None),
        P(None, "tensor"),
        P(),
        P(),
        P("expert", None, "tensor"),
        P("expert", "tensor", None),
        P("expert", None),
    )
    return jax.shard_map(
        on_device,
        mesh=mesh,
        in_specs=placed,
        out_specs=(
            P("expert", None),
            P("expert", None),
            P(),
            P(None, None, "tensor"),
            P("tensor", None),
            P(None, "tensor"),
            P(),
            P(),
            P("expert", None, "tensor"),
            P("expert", "tensor", None),
        ),
        check_vma=False,
    )
```

```python
import functools

import jax
import jax.numpy as jnp
from jax import lax
from jax.experimental import pallas as pl
from jax.experimental.pallas import tpu as pltpu
from jax.sharding import PartitionSpec as P

edge_list = (1, 2, 3, 4, 5, 6, 7, 8, 12, 16, 23, 32, 46, 64, 91)
tiny_eps = 1e-06
masked_score = -1e30
sum_chunks = 4
largest_logit = lax.Precision.HIGHEST


def offset_buckets(row_count):
    span = 2 * row_count
    places = jnp.arange(span, dtype=jnp.int32)
    offsets = jnp.where(places < row_count, -places, span - places)
    bounds = jnp.asarray(edge_list, dtype=jnp.int32)
    passed = jnp.sum((jnp.abs(offsets)[:, None] >= bounds[None, :]).astype(jnp.int32), axis=1)
    return passed + 16 * (offsets < 0).astype(jnp.int32)


def document_ids(lengths_row, row_count):
    places = jnp.arange(row_count, dtype=jnp.int32)
    endings = jnp.cumsum(lengths_row)
    return jnp.sum((places[:, None] >= endings[None, :]).astype(jnp.int32), axis=1)


def rms_scale(values, gain):
    return values * lax.rsqrt(jnp.mean(values * values, axis=-1, keepdims=True) + tiny_eps) * gain


def gelu_curve(values):
    return (
        0.5
        * values
        * (1.0 + jnp.tanh(0.7978845608 * (values + 0.044715 * values * values * values)))
    )


def softmax_rows(scores):
    top_score = jnp.max(scores, axis=-1, keepdims=True)
    raised = jnp.exp(scores - top_score)
    return raised / jnp.sum(raised, axis=-1, keepdims=True)


MESH = pl.DeviceIdType.MESH


def vmem():
    return pl.BlockSpec(memory_space=pltpu.VMEM)


def tensor_places():
    mine = lax.axis_index("tensor")
    core = mine % 2
    side = mine // 2
    return mine, core, side, side * 2 + (1 - core), (1 - side) * 2 + core


def greet(devices):
    barrier = pltpu.get_barrier_semaphore()
    for device in devices:
        pl.semaphore_signal(barrier, inc=1, device_id=device, device_id_type=MESH)
    pl.semaphore_wait(barrier, len(devices))


def remote(source, target, send_sem, recv_sem, device):
    return pltpu.make_async_remote_copy(
        src_ref=source,
        dst_ref=target,
        send_sem=send_sem,
        recv_sem=recv_sem,
        device_id=device,
        device_id_type=MESH,
    )


def tensor_sum_steps(x_ref, o_ref, near, chip, far, send_sem, recv_sem):
    _, core, _, sibling, across = tensor_places()
    half = x_ref.shape[0] // 2
    chunk = half // sum_chunks
    copies = []

    def rows_of(which, turn):
        return pl.ds(pl.multiple_of(which * half + turn * chunk, chunk), chunk)

    def begin(source, target, place, device):
        copy = remote(source, target, send_sem.at[place], recv_sem.at[place], {"tensor": device})
        copy.start()
        copies.append(copy)
        return copy

    first = [
        begin(x_ref.at[rows_of(1 - core, turn)], near.at[turn], turn, sibling)
        for turn in range(sum_chunks)
    ]
    yield
    second = []
    for turn in range(sum_chunks):
        first[turn].wait_recv()
        own = x_ref[rows_of(core, turn)].astype(jnp.float32)
        chip[turn] = (own + near[turn].astype(jnp.float32)).astype(chip.dtype)
        second.append(begin(chip.at[turn], far.at[turn], sum_chunks + turn, across))
    yield
    third = []
    for turn in range(sum_chunks):
        second[turn].wait_recv()
        own = rows_of(core, turn)
        o_ref[own] = chip[turn].astype(jnp.float32) + far[turn].astype(jnp.float32)
        third.append(begin(o_ref.at[own], o_ref.at[own], 2 * sum_chunks + turn, sibling))
    yield
    for copy in third:
        copy.wait_recv()
    for copy in copies:
        copy.wait_send()
    yield


def tensor_sum_scratch(rows, width):
    chunk = pltpu.VMEM((sum_chunks, rows // 2 // sum_chunks, width), jnp.bfloat16)
    sems = pltpu.SemaphoreType.DMA((3 * sum_chunks,))
    return [chunk, chunk, chunk, sems, sems]


def tensor_sum_kernel(*refs):
    _, _, _, sibling, across = tensor_places()
    greet([{"tensor": sibling}, {"tensor": across}])
    for _ in tensor_sum_steps(*refs):
        pass


def tensor_total(value, collective_id):
    rows, width = value.shape
    if lax.axis_size("tensor") != 4 or rows % (32 * sum_chunks):
        return lax.psum(value, "tensor")
    return pl.pallas_call(
        tensor_sum_kernel,
        out_shape=jax.ShapeDtypeStruct((rows, width), jnp.float32),
        in_specs=[vmem()],
        out_specs=vmem(),
        scratch_shapes=tensor_sum_scratch(rows, width),
        compiler_params=pltpu.CompilerParams(
            collective_id=collective_id, has_side_effects=True, vmem_limit_bytes=32 * 2**20
        ),
        cost_estimate=pl.CostEstimate(flops=0, bytes_accessed=30_000_000, transcendentals=0),
    )(value.astype(jnp.bfloat16))


def share_over_tensor(places, pieces, sems):
    mine, _, _, sibling, across = places
    across_send, across_recv, near_send, near_recv, pass_send, pass_recv = sems

    def begin(step):
        far = remote(
            pieces(mine, step),
            pieces(mine, step),
            across_send.at[step],
            across_recv.at[step],
            {"tensor": across},
        )
        close = remote(
            pieces(mine, step),
            pieces(mine, step),
            near_send.at[step],
            near_recv.at[step],
            {"tensor": sibling},
        )
        far.start()
        close.start()
        return far, close

    def forward(step):
        onward = remote(
            pieces(across, step),
            pieces(across, step),
            pass_send.at[step],
            pass_recv.at[step],
            {"tensor": sibling},
        )
        onward.start()
        return onward

    return begin, forward


def dispatch_kernel(groups, send_ref, o_ref, out_send, out_recv, *sems):
    here = lax.axis_index("expert")
    places = tensor_places()
    mine, _, _, sibling, across = places
    peers = [lax.rem(here + step, groups) for step in range(groups)]
    greet([{"expert": peer} for peer in peers[1:]] + [{"tensor": sibling}, {"tensor": across}])
    copies = [None]
    for step in range(1, groups):
        copy = remote(
            send_ref.at[peers[step]],
            o_ref.at[mine, here],
            out_send.at[step],
            out_recv.at[step],
            {"expert": peers[step]},
        )
        copy.start()
        copies.append(copy)
    o_ref[mine, here] = send_ref[here]

    def pieces(quarter, step):
        return o_ref.at[quarter, lax.rem(here + groups - step, groups)]

    begin, forward = share_over_tensor(places, pieces, sems)
    shared = []
    for step in range(groups):
        if step:
            copies[step].wait_recv()
        shared.append(begin(step))
    onward = []
    for step in range(groups):
        shared[step][0].wait_recv()
        onward.append(forward(step))
    for step in range(groups):
        if step:
            copies[step].wait_send()
        shared[step][0].wait_send()
        shared[step][1].wait()
        onward[step].wait()


def kernels_fit(part_rows):
    return lax.axis_size("tensor") == 4 and lax.axis_size("expert") <= 8 and part_rows % 16 == 0


def dispatch(send, collective_id):
    groups, part, width = send.shape
    if collective_id is None or not kernels_fit(part):
        received = lax.all_to_all(send, "expert", split_axis=0, concat_axis=0, tiled=True)
        return lax.all_gather(received, "tensor", axis=0, tiled=False)
    sems = pltpu.SemaphoreType.DMA((groups,))
    return pl.pallas_call(
        functools.partial(dispatch_kernel, groups),
        out_shape=jax.ShapeDtypeStruct((lax.axis_size("tensor"),) + send.shape, send.dtype),
        in_specs=[vmem()],
        out_specs=vmem(),
        scratch_shapes=[sems] * 8,
        compiler_params=pltpu.CompilerParams(
            collective_id=collective_id, has_side_effects=True, vmem_limit_bytes=32 * 2**20
        ),
        cost_estimate=pl.CostEstimate(flops=0, bytes_accessed=50_000_000, transcendentals=0),
    )(send)


def combine_kernel(groups, ahead_ref, back_ref, o_ref, near, chip, far, total, *sems):
    near_send, near_recv, far_send, far_recv, out_send, out_recv = sems[:6]
    here = lax.axis_index("expert")
    places = tensor_places()
    mine, core, side, sibling, across = places
    peers = [lax.rem(here + step, groups) for step in range(groups)]
    greet([{"expert": peer} for peer in peers[1:]] + [{"tensor": sibling}, {"tensor": across}])
    inputs = (ahead_ref, back_ref)
    sides = (1 - side, side)
    gather = []
    for kind in range(2):
        for turn in range(2):
            copy = remote(
                inputs[kind].at[sides[turn] * 2 + (1 - core)],
                near.at[2 * kind + turn],
                near_send.at[2 * kind + turn],
                near_recv.at[2 * kind + turn],
                {"tensor": sibling},
            )
            copy.start()
            gather.append(copy)
    crossing = []
    for kind in range(2):
        for turn in range(2):
            gather[2 * kind + turn].wait_recv()
            chip[2 * kind + turn] = (
                inputs[kind][sides[turn] * 2 + core].astype(jnp.float32)
                + near[2 * kind + turn].astype(jnp.float32)
            ).astype(chip.dtype)
            if turn == 0:
                copy = remote(
                    chip.at[2 * kind],
                    far.at[kind],
                    far_send.at[kind],
                    far_recv.at[kind],
                    {"tensor": across},
                )
                copy.start()
                crossing.append(copy)
    outgoing = []
    for kind in range(2):
        crossing[kind].wait_recv()
        total[kind] = (
            chip[2 * kind + 1].astype(jnp.float32) + far[kind].astype(jnp.float32)
        ).astype(total.dtype)
        outgoing.append(None)
        for step in range(1, groups):
            copy = remote(
                total.at[kind, peers[step]],
                o_ref.at[kind, mine, here],
                out_send.at[kind * groups + step],
                out_recv.at[kind * groups + step],
                {"expert": peers[step]},
            )
            copy.start()
            outgoing.append(copy)
        o_ref[kind, mine, here] = total[kind, here]

    def pieces(quarter, place):
        return o_ref.at[place // groups, quarter, lax.rem(here + groups - place % groups, groups)]

    begin, forward = share_over_tensor(places, pieces, sems[6:])
    shared = []
    for place in range(2 * groups):
        if place % groups:
            outgoing[place].wait_recv()
        shared.append(begin(place))
    onward = []
    for place in range(2 * groups):
        shared[place][0].wait_recv()
        onward.append(forward(place))
    for copy in gather + crossing:
        copy.wait_send()
    for place in range(2 * groups):
        if place % groups:
            outgoing[place].wait_send()
        shared[place][0].wait_send()
        shared[place][1].wait()
        onward[place].wait()


def combine(ahead, back, collective_id):
    quarters, groups, part, width = ahead.shape
    if not kernels_fit(part):
        both = jnp.stack([ahead, back], axis=1).astype(jnp.float32)
        mine = lax.psum_scatter(both, "tensor", scatter_dimension=0, tiled=False)
        received = lax.all_to_all(
            mine.astype(jnp.bfloat16), "expert", split_axis=1, concat_axis=1, tiled=True
        )
        return lax.all_gather(received, "tensor", axis=1, tiled=False)
    piece = (groups, part, width)
    one = pltpu.SemaphoreType.DMA((2 * groups,))
    return pl.pallas_call(
        functools.partial(combine_kernel, groups),
        out_shape=jax.ShapeDtypeStruct((2,) + ahead.shape, jnp.bfloat16),
        in_specs=[vmem(), vmem()],
        out_specs=vmem(),
        scratch_shapes=[
            pltpu.VMEM((4,) + piece, jnp.bfloat16),
            pltpu.VMEM((4,) + piece, jnp.bfloat16),
            pltpu.VMEM((2,) + piece, jnp.bfloat16),
            pltpu.VMEM((2,) + piece, jnp.bfloat16),
            pltpu.SemaphoreType.DMA((4,)),
            pltpu.SemaphoreType.DMA((4,)),
            pltpu.SemaphoreType.DMA((2,)),
            pltpu.SemaphoreType.DMA((2,)),
        ]
        + [one] * 8,
        compiler_params=pltpu.CompilerParams(
            collective_id=collective_id, has_side_effects=True, vmem_limit_bytes=40 * 2**20
        ),
        cost_estimate=pl.CostEstimate(flops=0, bytes_accessed=120_000_000, transcendentals=0),
    )(ahead, back)


def finish_kernel(
    groups, x_ref, unit_ref, big_ref, small_ref, o_ref, big_out, small_out, gain_out, *scratch
):
    (
        pair_buf,
        line_send,
        line_buf,
        small_buf,
        gain_buf,
        pair_sems,
        line_sems,
        spread_sems,
        pass_sems,
        small_sems,
        gain_sems,
    ) = scratch[:11]
    here = lax.axis_index("expert")
    _, _, _, sibling, across = tensor_places()
    lines = groups // 2
    place = here // 2
    lane = here % 2
    pair = place * 2 + (1 - lane)
    peers = [lax.rem(here + step, groups) for step in range(groups)]
    greet([{"expert": peer} for peer in peers[1:]] + [{"tensor": sibling}, {"tensor": across}])
    copies = []

    def begin(source, target, sems, index, device):
        copy = remote(source, target, sems.at[0, index], sems.at[1, index], {"expert": device})
        copy.start()
        copies.append(copy)
        return copy

    order = list(range(1, lines)) + [0]
    places = [lax.rem(place + step, lines) for step in range(lines)]
    pairs = {}
    for step in order:
        pairs[step] = begin(
            big_ref.at[places[step] * 2 + (1 - lane)], pair_buf.at[step], pair_sems, step, pair
        )
    steps = tensor_sum_steps(x_ref, o_ref, *scratch[11:])
    next(steps)
    smalls = [None]
    small_buf[here] = small_ref[...]
    for step in range(1, groups):
        smalls.append(
            begin(small_ref, small_buf.at[here], small_sems, step, peers[step])
        )
    next(steps)
    along = {}
    for step in order:
        pairs[step].wait_recv()
        line_send[step] = (
            big_ref[places[step] * 2 + lane].astype(jnp.float32)
            + pair_buf[step].astype(jnp.float32)
        ).astype(line_send.dtype)
        if step:
            along[step] = begin(
                line_send.at[step], line_buf.at[step], line_sems, step, places[step] * 2 + lane
            )
    next(steps)
    next(steps)
    gain = jnp.sum(o_ref[...] * unit_ref[...], axis=0, keepdims=True)
    gain_out[...] = jnp.broadcast_to(gain, gain_out.shape)
    gain_buf[here] = gain_out[...]
    gains = [None]
    for step in range(1, groups):
        gains.append(begin(gain_out, gain_buf.at[here], gain_sems, step, peers[step]))
    total = line_send[0].astype(jnp.float32)
    for step in range(1, lines):
        along[step].wait_recv()
        total = total + line_buf[step].astype(jnp.float32)
    big_out[here] = total.astype(big_out.dtype)
    spread = {}
    for step in order:
        device = places[step] * 2 + lane if step else pair
        spread[step] = begin(big_out.at[here], big_out.at[here], spread_sems, step, device)
    passed = []
    for step in range(1, lines):
        spread[step].wait_recv()
        came = lax.rem(place + lines - step, lines) * 2 + lane
        passed.append(begin(big_out.at[came], big_out.at[came], pass_sems, step, pair))
    for copy in smalls[1:] + gains[1:] + [spread[0]] + passed:
        copy.wait_recv()
    for copy in copies:
        copy.wait_send()
    small_sum = small_buf[0]
    gain_sum = gain_buf[0]
    for source in range(1, groups):
        small_sum = small_sum + small_buf[source]
        gain_sum = gain_sum + gain_buf[source]
    small_out[...] = small_sum
    gain_out[...] = gain_sum


def finish(partial, unit, large, small, collective_id):
    rows, width = partial.shape
    groups = lax.axis_size("expert")
    if (
        lax.axis_size("tensor") != 4
        or groups != 8
        or large.shape[0] % (16 * groups)
        or rows % (32 * sum_chunks)
    ):
        total = lax.psum(partial, "tensor")
        gain, small = lax.psum((jnp.sum(total * unit, axis=0), small), "expert")
        large = lax.psum(large.astype(jnp.bfloat16), "expert")
        return total, large.astype(jnp.float32), small, gain
    piece = (large.shape[0] // groups, width)
    lines = groups // 2
    few = pltpu.SemaphoreType.DMA((2, lines))
    many = pltpu.SemaphoreType.DMA((2, groups))
    gains = (8, width)
    total, large, small, gain = pl.pallas_call(
        functools.partial(finish_kernel, groups),
        out_shape=(
            jax.ShapeDtypeStruct((rows, width), jnp.float32),
            jax.ShapeDtypeStruct((groups,) + piece, jnp.bfloat16),
            jax.ShapeDtypeStruct(small.shape, jnp.float32),
            jax.ShapeDtypeStruct(gains, jnp.float32),
        ),
        in_specs=[vmem()] * 4,
        out_specs=(vmem(),) * 4,
        scratch_shapes=[
            pltpu.VMEM((lines,) + piece, jnp.bfloat16),
            pltpu.VMEM((lines,) + piece, jnp.bfloat16),
            pltpu.VMEM((lines,) + piece, jnp.bfloat16),
            pltpu.VMEM((groups,) + small.shape, jnp.float32),
            pltpu.VMEM((groups,) + gains, jnp.float32),
            few,
            few,
            few,
            few,
            many,
            many,
        ]
        + tensor_sum_scratch(rows, width),
        compiler_params=pltpu.CompilerParams(
            collective_id=collective_id, has_side_effects=True, vmem_limit_bytes=40 * 2**20
        ),
        cost_estimate=pl.CostEstimate(flops=0, bytes_accessed=100_000_000, transcendentals=0),
    )(partial.astype(jnp.bfloat16), unit, large.astype(jnp.bfloat16).reshape((groups,) + piece), small)
    return total, large.astype(jnp.float32).reshape(-1, width), small, gain[0]


def rows_dot(left, right):
    return lax.dot_general(
        left, right, (((1,), (1,)), ((), ())), preferred_element_type=jnp.float32
    )


def columns_dot(left, right):
    return lax.dot_general(
        left, right, (((0,), (0,)), ((), ())), preferred_element_type=jnp.float32
    )


def masked_scores(queries, keys_here, line, doc_column, doc_row, score_scale):
    row_count = queries.shape[0]
    bias = line
    while bias.shape[0] < row_count:
        bias = jnp.concatenate([bias, pltpu.roll(bias, bias.shape[0], 1)], axis=0)
    raw = rows_dot(queries, keys_here) * score_scale + bias[:, :row_count]
    return jnp.where(doc_column == doc_row, raw, masked_score)


def attention_kernel(heads, scale, qkv_ref, line_ref, column_ref, row_ref, mixed_ref, log_ref):
    size = qkv_ref.shape[2] // heads
    for head in range(heads):
        part = slice(head * size, head * size + size)
        scores = masked_scores(
            qkv_ref[0, :, part],
            qkv_ref[1, :, part],
            line_ref[head : head + 1, :],
            column_ref[...],
            row_ref[...],
            scale,
        )
        top_score = jnp.max(scores, axis=-1, keepdims=True)
        raised = jnp.exp(scores - top_score)
        totals = jnp.sum(raised, axis=-1, keepdims=True)
        soft = (raised / totals).astype(jnp.bfloat16)
        mixed_ref[:, part] = jnp.dot(
            soft, qkv_ref[2, :, part], preferred_element_type=jnp.float32
        ).astype(mixed_ref.dtype)
        log_ref[head] = top_score + jnp.log(totals)


def attention_back_kernel(
    heads, scale, qkv_ref, line_ref, column_ref, row_ref, log_ref, up_ref, grad_ref, sums_ref
):
    size = qkv_ref.shape[2] // heads
    row_count = qkv_ref.shape[1]
    for head in range(heads):
        part = slice(head * size, head * size + size)
        queries = qkv_ref[0, :, part]
        keys_here = qkv_ref[1, :, part]
        upstream = up_ref[:, part]
        scores = masked_scores(
            queries,
            keys_here,
            line_ref[head : head + 1, :],
            column_ref[...],
            row_ref[...],
            scale,
        )
        soft = jnp.exp(scores - log_ref[head])
        grad_soft = rows_dot(upstream, qkv_ref[2, :, part])
        centre = jnp.sum(soft * grad_soft, axis=-1, keepdims=True)
        grad_scores = (soft * (grad_soft - centre)).astype(jnp.bfloat16)
        grad_ref[2, :, part] = columns_dot(soft.astype(jnp.bfloat16), upstream).astype(
            grad_ref.dtype
        )
        grad_ref[0, :, part] = (
            jnp.dot(grad_scores, keys_here, preferred_element_type=jnp.float32) * scale
        ).astype(grad_ref.dtype)
        grad_ref[1, :, part] = (columns_dot(grad_scores, queries) * scale).astype(grad_ref.dtype)
        wide = grad_scores.astype(jnp.float32)
        wide = jnp.concatenate([wide, jnp.zeros_like(wide)], axis=1)
        while wide.shape[0] > 1:
            half = wide.shape[0] // 2
            wide = wide[:half] + pltpu.roll(wide[half:], 2 * row_count - half, 1)
        sums_ref[head : head + 1, :] = wide


def local_call(kernel, outs, args):
    return pl.pallas_call(
        kernel,
        out_shape=outs,
        in_specs=[vmem()] * len(args),
        out_specs=tuple(vmem() for _ in outs),
        compiler_params=pltpu.CompilerParams(vmem_limit_bytes=40 * 2**20),
        cost_estimate=pl.CostEstimate(
            flops=1_000_000_000, bytes_accessed=30_000_000, transcendentals=1_000_000
        ),
    )(*args)


def on_device(
    tokens,
    doc_lengths,
    routes,
    gain_first,
    projections,
    attention_out,
    relative_bias_table,
    gain_second,
    router_weight,
    expert_in,
    expert_out,
    cotangent,
):
    row_count = tokens.shape[0]
    model_width = tokens.shape[1]
    heads_here = relative_bias_table.shape[1]
    buckets_total = relative_bias_table.shape[0]
    width_here = projections.shape[2]
    head_size = width_here // heads_here
    experts_total = router_weight.shape[1]
    tensor_size = lax.axis_size("tensor")
    capacity = max(2, 2 * row_count // experts_total)
    part = capacity // tensor_size
    part_rows = experts_total * part
    score_scale = head_size ** (-0.5)
    quarter = lax.axis_index("tensor")

    route_column = routes[:, 0]
    chosen = route_column[:, None] == jnp.arange(experts_total, dtype=jnp.int32)[None, :]
    earlier = jnp.cumsum(chosen.astype(jnp.int32), axis=0) - 1
    slot = jnp.sum(jnp.where(chosen, earlier, 0), axis=1)
    place = (slot // part) * part_rows + route_column * part + slot % part
    own_place = place - quarter * part_rows
    send_pick = (
        jnp.arange(part_rows, dtype=jnp.int32)[:, None] == own_place[None, :]
    ).astype(jnp.bfloat16)
    take_pick = (
        place[:, None] == jnp.arange(tensor_size * part_rows, dtype=jnp.int32)[None, :]
    ).astype(jnp.bfloat16)

    def placed_rows(rows):
        picked_rows = jnp.dot(send_pick, rows, preferred_element_type=jnp.float32)
        return picked_rows.astype(jnp.bfloat16).reshape(experts_total, part, rows.shape[1])

    upstream_rows = dispatch(placed_rows(cotangent), None)

    token_float = tokens.astype(jnp.float32)
    normed_float, first_back = jax.vjp(rms_scale, token_float, gain_first)
    normed_first = normed_float.astype(jnp.bfloat16)
    projected = jnp.einsum(
        "nd,cdh->cnh", normed_first, projections, preferred_element_type=jnp.float32
    ).astype(jnp.bfloat16)
    bucket_pick = (
        jnp.arange(buckets_total, dtype=jnp.int32)[:, None] == offset_buckets(row_count)[None, :]
    ).astype(jnp.float32)
    bias_line = jnp.einsum("bh,bm->hm", relative_bias_table, bucket_pick, precision=largest_logit)
    documents = document_ids(doc_lengths[0], row_count)
    shared_args = (projected, bias_line, documents[:, None], documents[None, :])
    mixed_heads, log_total = local_call(
        functools.partial(attention_kernel, heads_here, score_scale),
        (
            jax.ShapeDtypeStruct((row_count, width_here), jnp.bfloat16),
            jax.ShapeDtypeStruct((heads_here, row_count, 1), jnp.float32),
        ),
        shared_args,
    )
    after_attention = token_float + tensor_total(
        jnp.dot(mixed_heads, attention_out, preferred_element_type=jnp.float32), 0
    )
    second_float, second_back = jax.vjp(rms_scale, after_attention, gain_second)
    normed_second = second_float.astype(jnp.bfloat16)
    normed_wide = normed_second.astype(jnp.float32)
    router_float = router_weight.astype(jnp.float32)
    router_probs = softmax_rows(jnp.dot(normed_wide, router_float, precision=largest_logit))
    gate_value = jnp.sum(jnp.where(chosen, router_probs, 0.0), axis=1)

    gate_high = lax.reduce_precision(gate_value, 8, 7)
    gate_rest = gate_value - gate_high
    gate_middle = lax.reduce_precision(gate_rest, 8, 7)
    gate_terms = jnp.stack([gate_high, gate_middle, gate_rest - gate_middle], axis=1)
    gate_columns = jnp.pad(gate_terms.astype(jnp.bfloat16), ((0, 0), (0, 125)))
    arrived = dispatch(placed_rows(jnp.concatenate([normed_second, gate_columns], axis=1)), 1)
    arrived = arrived.reshape(tensor_size * part_rows, model_width + 128)
    expert_rows = arrived[:, :model_width]
    row_gates = jnp.sum(
        arrived[:, model_width : model_width + 3].astype(jnp.float32), axis=1, keepdims=True
    )
    grad_rows = (
        row_gates * upstream_rows.reshape(expert_rows.shape).astype(jnp.float32)
    ).astype(jnp.bfloat16)
    weight_in = expert_in[0]
    weight_out = expert_out[0]
    pre_active = jnp.dot(expert_rows, weight_in, preferred_element_type=jnp.float32)
    hidden_float, gelu_back = jax.vjp(gelu_curve, pre_active)
    hidden_units = hidden_float.astype(jnp.bfloat16)
    partial_rows = jnp.dot(hidden_units, weight_out, preferred_element_type=jnp.float32)
    grad_hidden = rows_dot(grad_rows, weight_out)
    grad_pre = gelu_back(grad_hidden)[0].astype(jnp.bfloat16)
    grad_inputs = rows_dot(grad_pre, weight_in)
    blocks = (tensor_size, experts_total, part, model_width)
    returned = combine(
        partial_rows.astype(jnp.bfloat16).reshape(blocks),
        grad_inputs.astype(jnp.bfloat16).reshape(blocks),
        2,
    ).reshape(2, tensor_size * part_rows, model_width)
    grad_expert_out = columns_dot(hidden_units, grad_rows)[None]
    grad_expert_in = columns_dot(expert_rows, grad_pre)[None]
    picked = jnp.dot(take_pick, returned[0], preferred_element_type=jnp.float32)
    grad_from_experts = jnp.dot(take_pick, returned[1], preferred_element_type=jnp.float32)
    layer_output = (after_attention + gate_value[:, None] * picked).astype(jnp.bfloat16)
    upstream = cotangent.astype(jnp.float32)
    grad_gate = jnp.sum(upstream * picked, axis=1)
    grad_logits = router_probs * (
        jnp.where(chosen, grad_gate[:, None], 0.0) - (gate_value * grad_gate)[:, None]
    )
    grad_router = jnp.dot(normed_wide.T, grad_logits, precision=largest_logit)
    grad_normed_second = grad_from_experts + jnp.dot(
        grad_logits, router_float.T, precision=largest_logit
    )
    grad_after, grad_gain_second = second_back(grad_normed_second)
    grad_residual = upstream + grad_after
    grad_attention_low = grad_residual.astype(jnp.bfloat16)
    grad_attention_out = columns_dot(mixed_heads, grad_attention_low)
    grad_mixed = rows_dot(grad_attention_low, attention_out).astype(jnp.bfloat16)
    grad_projected, offset_sums = local_call(
        functools.partial(attention_back_kernel, heads_here, score_scale),
        (
            jax.ShapeDtypeStruct((3, row_count, width_here), jnp.bfloat16),
            jax.ShapeDtypeStruct((heads_here, 2 * row_count), jnp.float32),
        ),
        shared_args + (log_total, grad_mixed),
    )
    grad_position_table = jnp.einsum(
        "hm,bm->bh", offset_sums, bucket_pick, precision=largest_logit
    )
    grad_projections = jnp.einsum(
        "cnh,nd->chd", grad_projected, normed_first, preferred_element_type=jnp.float32
    ).reshape(3 * width_here, model_width)
    first_scale = lax.rsqrt(
        jnp.mean(token_float * token_float, axis=-1, keepdims=True) + tiny_eps
    )
    table_row = jnp.pad(
        grad_position_table.reshape(1, -1),
        ((0, 0), (0, model_width - buckets_total * heads_here)),
    )
    small = jnp.concatenate([grad_gain_second[None], table_row, grad_router.T], axis=0)
    small = jnp.pad(small, ((0, -small.shape[0] % 16), (0, 0)))
    grad_normed_first, large, small, grad_gain_first = finish(
        jnp.einsum("cnh,cdh->nd", grad_projected, projections, preferred_element_type=jnp.float32),
        token_float * first_scale,
        jnp.concatenate([grad_projections, grad_attention_out], axis=0),
        small,
        3,
    )
    grad_first_in = first_back(grad_normed_first)[0]
    grad_tokens = grad_residual + grad_first_in
    return (
        layer_output,
        grad_tokens,
        grad_gain_first,
        large[: 3 * width_here].reshape(3, width_here, model_width).transpose(0, 2, 1),
        large[3 * width_here :],
        small[1, : buckets_total * heads_here].reshape(buckets_total, heads_here),
        small[0],
        small[2 : 2 + experts_total].T,
        grad_expert_in,
        grad_expert_out,
    )


def solution(mesh):
    placed = (
        P("expert", None),
        P("expert", None),
        P("expert", None),
        P(),
        P(None, None, "tensor"),
        P("tensor", None),
        P(None, "tensor"),
        P(),
        P(),
        P("expert", None, "tensor"),
        P("expert", "tensor", None),
        P("expert", None),
    )
    return jax.shard_map(
        on_device,
        mesh=mesh,
        in_specs=placed,
        out_specs=(
            P("expert", None),
            P("expert", None),
            P(),
            P(None, None, "tensor"),
            P("tensor", None),
            P(None, "tensor"),
            P(),
            P(),
            P("expert", None, "tensor"),
            P("expert", "tensor", None),
        ),
        check_vma=False,
    )
```

```python
import functools

import jax
import jax.numpy as jnp
from jax import lax
from jax.experimental import pallas as pl
from jax.experimental.pallas import tpu as pltpu
from jax.sharding import PartitionSpec as P

edge_list = (1, 2, 3, 4, 5, 6, 7, 8, 12, 16, 23, 32, 46, 64, 91)
tiny_eps = 1e-06
masked_score = -1e30
sum_chunks = 4
largest_logit = lax.Precision.HIGHEST


def offset_buckets(row_count):
    span = 2 * row_count
    places = jnp.arange(span, dtype=jnp.int32)
    offsets = jnp.where(places < row_count, -places, span - places)
    bounds = jnp.asarray(edge_list, dtype=jnp.int32)
    passed = jnp.sum((jnp.abs(offsets)[:, None] >= bounds[None, :]).astype(jnp.int32), axis=1)
    return passed + 16 * (offsets < 0).astype(jnp.int32)


def document_ids(lengths_row, row_count):
    places = jnp.arange(row_count, dtype=jnp.int32)
    endings = jnp.cumsum(lengths_row)
    return jnp.sum((places[:, None] >= endings[None, :]).astype(jnp.int32), axis=1)


def rms_scale(values, gain):
    return values * lax.rsqrt(jnp.mean(values * values, axis=-1, keepdims=True) + tiny_eps) * gain


def gelu_curve(values):
    return (
        0.5
        * values
        * (1.0 + jnp.tanh(0.7978845608 * (values + 0.044715 * values * values * values)))
    )


def softmax_rows(scores):
    top_score = jnp.max(scores, axis=-1, keepdims=True)
    raised = jnp.exp(scores - top_score)
    return raised / jnp.sum(raised, axis=-1, keepdims=True)


MESH = pl.DeviceIdType.MESH


def vmem():
    return pl.BlockSpec(memory_space=pltpu.VMEM)


def tensor_places():
    mine = lax.axis_index("tensor")
    core = mine % 2
    side = mine // 2
    return mine, core, side, side * 2 + (1 - core), (1 - side) * 2 + core


def greet(devices):
    barrier = pltpu.get_barrier_semaphore()
    for device in devices:
        pl.semaphore_signal(barrier, inc=1, device_id=device, device_id_type=MESH)
    pl.semaphore_wait(barrier, len(devices))


def remote(source, target, send_sem, recv_sem, device):
    return pltpu.make_async_remote_copy(
        src_ref=source,
        dst_ref=target,
        send_sem=send_sem,
        recv_sem=recv_sem,
        device_id=device,
        device_id_type=MESH,
    )


def tensor_sum_steps(x_ref, o_ref, near, chip, far, send_sem, recv_sem):
    _, core, _, sibling, across = tensor_places()
    half = x_ref.shape[0] // 2
    chunk = half // sum_chunks
    copies = []

    def rows_of(which, turn):
        return pl.ds(pl.multiple_of(which * half + turn * chunk, chunk), chunk)

    def begin(source, target, place, device):
        copy = remote(source, target, send_sem.at[place], recv_sem.at[place], {"tensor": device})
        copy.start()
        copies.append(copy)
        return copy

    first = [
        begin(x_ref.at[rows_of(1 - core, turn)], near.at[turn], turn, sibling)
        for turn in range(sum_chunks)
    ]
    yield
    second = []
    for turn in range(sum_chunks):
        first[turn].wait_recv()
        own = x_ref[rows_of(core, turn)].astype(jnp.float32)
        chip[turn] = (own + near[turn].astype(jnp.float32)).astype(chip.dtype)
        second.append(begin(chip.at[turn], far.at[turn], sum_chunks + turn, across))
    yield
    third = []
    for turn in range(sum_chunks):
        second[turn].wait_recv()
        own = rows_of(core, turn)
        o_ref[own] = chip[turn].astype(jnp.float32) + far[turn].astype(jnp.float32)
        third.append(begin(o_ref.at[own], o_ref.at[own], 2 * sum_chunks + turn, sibling))
    yield
    for copy in third:
        copy.wait_recv()
    for copy in copies:
        copy.wait_send()
    yield


def tensor_sum_scratch(rows, width):
    chunk = pltpu.VMEM((sum_chunks, rows // 2 // sum_chunks, width), jnp.bfloat16)
    sems = pltpu.SemaphoreType.DMA((3 * sum_chunks,))
    return [chunk, chunk, chunk, sems, sems]


def tensor_sum_kernel(*refs):
    _, _, _, sibling, across = tensor_places()
    greet([{"tensor": sibling}, {"tensor": across}])
    for _ in tensor_sum_steps(*refs):
        pass


def tensor_total(value, collective_id):
    rows, width = value.shape
    if lax.axis_size("tensor") != 4 or rows % (32 * sum_chunks):
        return lax.psum(value, "tensor")
    return pl.pallas_call(
        tensor_sum_kernel,
        out_shape=jax.ShapeDtypeStruct((rows, width), jnp.float32),
        in_specs=[vmem()],
        out_specs=vmem(),
        scratch_shapes=tensor_sum_scratch(rows, width),
        compiler_params=pltpu.CompilerParams(
            collective_id=collective_id, has_side_effects=True, vmem_limit_bytes=32 * 2**20
        ),
        cost_estimate=pl.CostEstimate(flops=0, bytes_accessed=30_000_000, transcendentals=0),
    )(value.astype(jnp.bfloat16))


def share_over_tensor(places, pieces, sems):
    mine, _, _, sibling, across = places
    across_send, across_recv, near_send, near_recv, pass_send, pass_recv = sems

    def begin(step):
        far = remote(
            pieces(mine, step),
            pieces(mine, step),
            across_send.at[step],
            across_recv.at[step],
            {"tensor": across},
        )
        close = remote(
            pieces(mine, step),
            pieces(mine, step),
            near_send.at[step],
            near_recv.at[step],
            {"tensor": sibling},
        )
        far.start()
        close.start()
        return far, close

    def forward(step):
        onward = remote(
            pieces(across, step),
            pieces(across, step),
            pass_send.at[step],
            pass_recv.at[step],
            {"tensor": sibling},
        )
        onward.start()
        return onward

    return begin, forward


def dispatch_kernel(groups, send_ref, o_ref, out_send, out_recv, *sems):
    here = lax.axis_index("expert")
    places = tensor_places()
    mine, _, _, sibling, across = places
    peers = [lax.rem(here + step, groups) for step in range(groups)]
    greet([{"expert": peer} for peer in peers[1:]] + [{"tensor": sibling}, {"tensor": across}])
    copies = [None]
    for step in range(1, groups):
        copy = remote(
            send_ref.at[peers[step]],
            o_ref.at[mine, here],
            out_send.at[step],
            out_recv.at[step],
            {"expert": peers[step]},
        )
        copy.start()
        copies.append(copy)
    o_ref[mine, here] = send_ref[here]

    def pieces(quarter, step):
        return o_ref.at[quarter, lax.rem(here + groups - step, groups)]

    begin, forward = share_over_tensor(places, pieces, sems)
    shared = []
    for step in range(groups):
        if step:
            copies[step].wait_recv()
        shared.append(begin(step))
    onward = []
    for step in range(groups):
        shared[step][0].wait_recv()
        onward.append(forward(step))
    for step in range(groups):
        if step:
            copies[step].wait_send()
        shared[step][0].wait_send()
        shared[step][1].wait()
        onward[step].wait()


def kernels_fit(part_rows):
    return lax.axis_size("tensor") == 4 and lax.axis_size("expert") <= 8 and part_rows % 16 == 0


def dispatch(send, collective_id):
    groups, part, width = send.shape
    if not kernels_fit(part):
        received = lax.all_to_all(send, "expert", split_axis=0, concat_axis=0, tiled=True)
        return lax.all_gather(received, "tensor", axis=0, tiled=False)
    sems = pltpu.SemaphoreType.DMA((groups,))
    return pl.pallas_call(
        functools.partial(dispatch_kernel, groups),
        out_shape=jax.ShapeDtypeStruct((lax.axis_size("tensor"),) + send.shape, send.dtype),
        in_specs=[vmem()],
        out_specs=vmem(),
        scratch_shapes=[sems] * 8,
        compiler_params=pltpu.CompilerParams(
            collective_id=collective_id, has_side_effects=True, vmem_limit_bytes=32 * 2**20
        ),
        cost_estimate=pl.CostEstimate(flops=0, bytes_accessed=50_000_000, transcendentals=0),
    )(send)


def combine_kernel(groups, ahead_ref, back_ref, o_ref, near, chip, far, total, *sems):
    near_send, near_recv, far_send, far_recv, out_send, out_recv = sems[:6]
    here = lax.axis_index("expert")
    places = tensor_places()
    mine, core, side, sibling, across = places
    peers = [lax.rem(here + step, groups) for step in range(groups)]
    greet([{"expert": peer} for peer in peers[1:]] + [{"tensor": sibling}, {"tensor": across}])
    inputs = (ahead_ref, back_ref)
    sides = (1 - side, side)
    gather = []
    for kind in range(2):
        for turn in range(2):
            copy = remote(
                inputs[kind].at[sides[turn] * 2 + (1 - core)],
                near.at[2 * kind + turn],
                near_send.at[2 * kind + turn],
                near_recv.at[2 * kind + turn],
                {"tensor": sibling},
            )
            copy.start()
            gather.append(copy)
    crossing = []
    for kind in range(2):
        for turn in range(2):
            gather[2 * kind + turn].wait_recv()
            chip[2 * kind + turn] = (
                inputs[kind][sides[turn] * 2 + core].astype(jnp.float32)
                + near[2 * kind + turn].astype(jnp.float32)
            ).astype(chip.dtype)
            if turn == 0:
                copy = remote(
                    chip.at[2 * kind],
                    far.at[kind],
                    far_send.at[kind],
                    far_recv.at[kind],
                    {"tensor": across},
                )
                copy.start()
                crossing.append(copy)
    outgoing = []
    for kind in range(2):
        crossing[kind].wait_recv()
        total[kind] = (
            chip[2 * kind + 1].astype(jnp.float32) + far[kind].astype(jnp.float32)
        ).astype(total.dtype)
        outgoing.append(None)
        for step in range(1, groups):
            copy = remote(
                total.at[kind, peers[step]],
                o_ref.at[kind, mine, here],
                out_send.at[kind * groups + step],
                out_recv.at[kind * groups + step],
                {"expert": peers[step]},
            )
            copy.start()
            outgoing.append(copy)
        o_ref[kind, mine, here] = total[kind, here]

    def pieces(quarter, place):
        return o_ref.at[place // groups, quarter, lax.rem(here + groups - place % groups, groups)]

    begin, forward = share_over_tensor(places, pieces, sems[6:])
    shared = []
    for place in range(2 * groups):
        if place % groups:
            outgoing[place].wait_recv()
        shared.append(begin(place))
    onward = []
    for place in range(2 * groups):
        shared[place][0].wait_recv()
        onward.append(forward(place))
    for copy in gather + crossing:
        copy.wait_send()
    for place in range(2 * groups):
        if place % groups:
            outgoing[place].wait_send()
        shared[place][0].wait_send()
        shared[place][1].wait()
        onward[place].wait()


def combine(ahead, back, collective_id):
    quarters, groups, part, width = ahead.shape
    if not kernels_fit(part):
        both = jnp.stack([ahead, back], axis=1).astype(jnp.float32)
        mine = lax.psum_scatter(both, "tensor", scatter_dimension=0, tiled=False)
        received = lax.all_to_all(
            mine.astype(jnp.bfloat16), "expert", split_axis=1, concat_axis=1, tiled=True
        )
        return lax.all_gather(received, "tensor", axis=1, tiled=False)
    piece = (groups, part, width)
    one = pltpu.SemaphoreType.DMA((2 * groups,))
    return pl.pallas_call(
        functools.partial(combine_kernel, groups),
        out_shape=jax.ShapeDtypeStruct((2,) + ahead.shape, jnp.bfloat16),
        in_specs=[vmem(), vmem()],
        out_specs=vmem(),
        scratch_shapes=[
            pltpu.VMEM((4,) + piece, jnp.bfloat16),
            pltpu.VMEM((4,) + piece, jnp.bfloat16),
            pltpu.VMEM((2,) + piece, jnp.bfloat16),
            pltpu.VMEM((2,) + piece, jnp.bfloat16),
            pltpu.SemaphoreType.DMA((4,)),
            pltpu.SemaphoreType.DMA((4,)),
            pltpu.SemaphoreType.DMA((2,)),
            pltpu.SemaphoreType.DMA((2,)),
        ]
        + [one] * 8,
        compiler_params=pltpu.CompilerParams(
            collective_id=collective_id, has_side_effects=True, vmem_limit_bytes=40 * 2**20
        ),
        cost_estimate=pl.CostEstimate(flops=0, bytes_accessed=120_000_000, transcendentals=0),
    )(ahead, back)


def finish_kernel(
    groups, x_ref, unit_ref, big_ref, small_ref, o_ref, big_out, small_out, *scratch
):
    (
        pair_buf,
        line_send,
        line_buf,
        small_send,
        small_pair,
        small_buf,
        pair_sems,
        line_sems,
        spread_sems,
        pass_sems,
        small_sems,
    ) = scratch[:11]
    here = lax.axis_index("expert")
    _, _, _, sibling, across = tensor_places()
    lines = groups // 2
    place = here // 2
    lane = here % 2
    pair = place * 2 + (1 - lane)
    places = [lax.rem(place + step, lines) for step in range(lines)]
    friends = [pair] + [places[step] * 2 + lane for step in range(1, lines)]
    greet([{"expert": friend} for friend in friends] + [{"tensor": sibling}, {"tensor": across}])
    copies = []

    def begin(source, target, sems, index, device):
        copy = remote(source, target, sems.at[0, index], sems.at[1, index], {"expert": device})
        copy.start()
        copies.append(copy)
        return copy

    order = list(range(1, lines)) + [0]
    pairs = {}
    for step in order:
        pairs[step] = begin(
            big_ref.at[places[step] * 2 + (1 - lane)], pair_buf.at[step], pair_sems, step, pair
        )
    steps = tensor_sum_steps(x_ref, o_ref, *scratch[11:])
    next(steps)
    next(steps)
    along = {}
    for step in order:
        pairs[step].wait_recv()
        line_send[step] = (
            big_ref[places[step] * 2 + lane].astype(jnp.float32)
            + pair_buf[step].astype(jnp.float32)
        ).astype(line_send.dtype)
        if step:
            along[step] = begin(
                line_send.at[step], line_buf.at[step], line_sems, step, places[step] * 2 + lane
            )
    next(steps)
    next(steps)
    gain = jnp.sum(o_ref[...] * unit_ref[...], axis=0, keepdims=True)
    last = lax.broadcasted_iota(jnp.int32, small_ref.shape, 0) == small_ref.shape[0] - 1
    small_send[0] = jnp.where(last, gain, small_ref[...])
    small_first = begin(small_send.at[0], small_pair, small_sems, 0, pair)
    total = line_send[0].astype(jnp.float32)
    for step in range(1, lines):
        along[step].wait_recv()
        total = total + line_buf[step].astype(jnp.float32)
    big_out[here] = total.astype(big_out.dtype)
    spread = {}
    for step in order:
        device = places[step] * 2 + lane if step else pair
        spread[step] = begin(big_out.at[here], big_out.at[here], spread_sems, step, device)
    small_first.wait_recv()
    small_send[1] = small_send[0] + small_pair[...]
    small_buf[place] = small_send[1]
    smalls = [
        begin(small_send.at[1], small_buf.at[place], small_sems, step, friends[step])
        for step in range(1, lines)
    ]
    passed = []
    for step in range(1, lines):
        spread[step].wait_recv()
        came = lax.rem(place + lines - step, lines) * 2 + lane
        passed.append(begin(big_out.at[came], big_out.at[came], pass_sems, step, pair))
    for copy in smalls + [spread[0]] + passed:
        copy.wait_recv()
    for copy in copies:
        copy.wait_send()
    small_sum = small_buf[0]
    for source in range(1, lines):
        small_sum = small_sum + small_buf[source]
    small_out[...] = small_sum


def finish(partial, unit, large, small, collective_id):
    rows, width = partial.shape
    groups = lax.axis_size("expert")
    if (
        lax.axis_size("tensor") != 4
        or groups != 8
        or large.shape[0] % (16 * groups)
        or rows % (32 * sum_chunks)
    ):
        total = lax.psum(partial, "tensor")
        gain, small = lax.psum((jnp.sum(total * unit, axis=0), small), "expert")
        large = lax.psum(large.astype(jnp.bfloat16), "expert")
        return total, large.astype(jnp.float32), small, gain
    piece = (large.shape[0] // groups, width)
    lines = groups // 2
    few = pltpu.SemaphoreType.DMA((2, lines))
    total, large, small = pl.pallas_call(
        functools.partial(finish_kernel, groups),
        out_shape=(
            jax.ShapeDtypeStruct((rows, width), jnp.float32),
            jax.ShapeDtypeStruct((groups,) + piece, jnp.bfloat16),
            jax.ShapeDtypeStruct(small.shape, jnp.float32),
        ),
        in_specs=[vmem()] * 4,
        out_specs=(vmem(),) * 3,
        scratch_shapes=[
            pltpu.VMEM((lines,) + piece, jnp.bfloat16),
            pltpu.VMEM((lines,) + piece, jnp.bfloat16),
            pltpu.VMEM((lines,) + piece, jnp.bfloat16),
            pltpu.VMEM((2,) + small.shape, jnp.float32),
            pltpu.VMEM(small.shape, jnp.float32),
            pltpu.VMEM((lines,) + small.shape, jnp.float32),
            few,
            few,
            few,
            few,
            few,
        ]
        + tensor_sum_scratch(rows, width),
        compiler_params=pltpu.CompilerParams(
            collective_id=collective_id, has_side_effects=True, vmem_limit_bytes=40 * 2**20
        ),
        cost_estimate=pl.CostEstimate(flops=0, bytes_accessed=100_000_000, transcendentals=0),
    )(partial.astype(jnp.bfloat16), unit, large.astype(jnp.bfloat16).reshape((groups,) + piece), small)
    return total, large.astype(jnp.float32).reshape(-1, width), small, small[-1]


def rows_dot(left, right):
    return lax.dot_general(
        left, right, (((1,), (1,)), ((), ())), preferred_element_type=jnp.float32
    )


def columns_dot(left, right):
    return lax.dot_general(
        left, right, (((0,), (0,)), ((), ())), preferred_element_type=jnp.float32
    )


def masked_scores(queries, keys_here, line, doc_column, doc_row, score_scale):
    row_count = queries.shape[0]
    bias = line
    while bias.shape[0] < row_count:
        bias = jnp.concatenate([bias, pltpu.roll(bias, bias.shape[0], 1)], axis=0)
    raw = rows_dot(queries, keys_here) * score_scale + bias[:, :row_count]
    return jnp.where(doc_column == doc_row, raw, masked_score)


def attention_kernel(heads, scale, qkv_ref, line_ref, column_ref, row_ref, mixed_ref, log_ref):
    size = qkv_ref.shape[2] // heads
    for head in range(heads):
        part = slice(head * size, head * size + size)
        scores = masked_scores(
            qkv_ref[0, :, part],
            qkv_ref[1, :, part],
            line_ref[head : head + 1, :],
            column_ref[...],
            row_ref[...],
            scale,
        )
        top_score = jnp.max(scores, axis=-1, keepdims=True)
        raised = jnp.exp(scores - top_score)
        totals = jnp.sum(raised, axis=-1, keepdims=True)
        soft = (raised / totals).astype(jnp.bfloat16)
        mixed_ref[:, part] = jnp.dot(
            soft, qkv_ref[2, :, part], preferred_element_type=jnp.float32
        ).astype(mixed_ref.dtype)
        log_ref[head] = top_score + jnp.log(totals)


def attention_back_kernel(
    heads, scale, qkv_ref, line_ref, column_ref, row_ref, log_ref, up_ref, grad_ref, sums_ref
):
    size = qkv_ref.shape[2] // heads
    row_count = qkv_ref.shape[1]
    for head in range(heads):
        part = slice(head * size, head * size + size)
        queries = qkv_ref[0, :, part]
        keys_here = qkv_ref[1, :, part]
        upstream = up_ref[:, part]
        scores = masked_scores(
            queries,
            keys_here,
            line_ref[head : head + 1, :],
            column_ref[...],
            row_ref[...],
            scale,
        )
        soft = jnp.exp(scores - log_ref[head])
        grad_soft = rows_dot(upstream, qkv_ref[2, :, part])
        centre = jnp.sum(soft * grad_soft, axis=-1, keepdims=True)
        grad_scores = (soft * (grad_soft - centre)).astype(jnp.bfloat16)
        grad_ref[2, :, part] = columns_dot(soft.astype(jnp.bfloat16), upstream).astype(
            grad_ref.dtype
        )
        grad_ref[0, :, part] = (
            jnp.dot(grad_scores, keys_here, preferred_element_type=jnp.float32) * scale
        ).astype(grad_ref.dtype)
        grad_ref[1, :, part] = (columns_dot(grad_scores, queries) * scale).astype(grad_ref.dtype)
        wide = grad_scores.astype(jnp.float32)
        wide = jnp.concatenate([wide, jnp.zeros_like(wide)], axis=1)
        while wide.shape[0] > 1:
            half = wide.shape[0] // 2
            wide = wide[:half] + pltpu.roll(wide[half:], 2 * row_count - half, 1)
        sums_ref[head : head + 1, :] = wide


def local_call(kernel, outs, args):
    return pl.pallas_call(
        kernel,
        out_shape=outs,
        in_specs=[vmem()] * len(args),
        out_specs=tuple(vmem() for _ in outs),
        compiler_params=pltpu.CompilerParams(vmem_limit_bytes=40 * 2**20),
        cost_estimate=pl.CostEstimate(
            flops=1_000_000_000, bytes_accessed=30_000_000, transcendentals=1_000_000
        ),
    )(*args)


def on_device(
    tokens,
    doc_lengths,
    routes,
    gain_first,
    projections,
    attention_out,
    relative_bias_table,
    gain_second,
    router_weight,
    expert_in,
    expert_out,
    cotangent,
):
    row_count = tokens.shape[0]
    model_width = tokens.shape[1]
    heads_here = relative_bias_table.shape[1]
    buckets_total = relative_bias_table.shape[0]
    width_here = projections.shape[2]
    head_size = width_here // heads_here
    experts_total = router_weight.shape[1]
    tensor_size = lax.axis_size("tensor")
    capacity = max(2, 2 * row_count // experts_total)
    part = capacity // tensor_size
    part_rows = experts_total * part
    score_scale = head_size ** (-0.5)
    quarter = lax.axis_index("tensor")

    route_column = routes[:, 0]
    chosen = route_column[:, None] == jnp.arange(experts_total, dtype=jnp.int32)[None, :]
    earlier = jnp.cumsum(chosen.astype(jnp.int32), axis=0) - 1
    slot = jnp.sum(jnp.where(chosen, earlier, 0), axis=1)
    place = (slot // part) * part_rows + route_column * part + slot % part
    own_place = place - quarter * part_rows
    send_pick = (
        jnp.arange(part_rows, dtype=jnp.int32)[:, None] == own_place[None, :]
    ).astype(jnp.bfloat16)
    take_pick = (
        place[:, None] == jnp.arange(tensor_size * part_rows, dtype=jnp.int32)[None, :]
    ).astype(jnp.bfloat16)

    def placed_rows(rows):
        picked_rows = jnp.dot(send_pick, rows, preferred_element_type=jnp.float32)
        return picked_rows.astype(jnp.bfloat16).reshape(experts_total, part, rows.shape[1])

    slot_pick = (
        jnp.arange(experts_total * capacity, dtype=jnp.int32)[:, None]
        == (route_column * capacity + slot)[None, :]
    ).astype(jnp.bfloat16)
    upstream_slots = (
        jnp.dot(slot_pick, cotangent, preferred_element_type=jnp.float32)
        .astype(jnp.bfloat16)
        .reshape(experts_total, capacity, model_width)
    )
    upstream_rows = (
        lax.all_to_all(upstream_slots, "expert", split_axis=0, concat_axis=0, tiled=True)
        .reshape(experts_total, tensor_size, part, model_width)
        .transpose(1, 0, 2, 3)
    )

    token_float = tokens.astype(jnp.float32)
    normed_float, first_back = jax.vjp(rms_scale, token_float, gain_first)
    normed_first = normed_float.astype(jnp.bfloat16)
    projected = jnp.einsum(
        "nd,cdh->cnh", normed_first, projections, preferred_element_type=jnp.float32
    ).astype(jnp.bfloat16)
    bucket_pick = (
        jnp.arange(buckets_total, dtype=jnp.int32)[:, None] == offset_buckets(row_count)[None, :]
    ).astype(jnp.float32)
    bias_line = jnp.einsum("bh,bm->hm", relative_bias_table, bucket_pick, precision=largest_logit)
    documents = document_ids(doc_lengths[0], row_count)
    shared_args = (projected, bias_line, documents[:, None], documents[None, :])
    mixed_heads, log_total = local_call(
        functools.partial(attention_kernel, heads_here, score_scale),
        (
            jax.ShapeDtypeStruct((row_count, width_here), jnp.bfloat16),
            jax.ShapeDtypeStruct((heads_here, row_count, 1), jnp.float32),
        ),
        shared_args,
    )
    after_attention = token_float + tensor_total(
        jnp.dot(mixed_heads, attention_out, preferred_element_type=jnp.float32), 0
    )
    second_float, second_back = jax.vjp(rms_scale, after_attention, gain_second)
    normed_second = second_float.astype(jnp.bfloat16)
    normed_wide = normed_second.astype(jnp.float32)
    router_float = router_weight.astype(jnp.float32)
    router_probs = softmax_rows(jnp.dot(normed_wide, router_float, precision=largest_logit))
    gate_value = jnp.sum(jnp.where(chosen, router_probs, 0.0), axis=1)

    gate_high = lax.reduce_precision(gate_value, 8, 7)
    gate_rest = gate_value - gate_high
    gate_middle = lax.reduce_precision(gate_rest, 8, 7)
    gate_terms = jnp.stack([gate_high, gate_middle, gate_rest - gate_middle], axis=1)
    gate_columns = jnp.pad(gate_terms.astype(jnp.bfloat16), ((0, 0), (0, 125)))
    arrived = dispatch(placed_rows(jnp.concatenate([normed_second, gate_columns], axis=1)), 1)
    arrived = arrived.reshape(tensor_size * part_rows, model_width + 128)
    expert_rows = arrived[:, :model_width]
    row_gates = jnp.sum(
        arrived[:, model_width : model_width + 3].astype(jnp.float32), axis=1, keepdims=True
    )
    grad_rows = (
        row_gates * upstream_rows.reshape(expert_rows.shape).astype(jnp.float32)
    ).astype(jnp.bfloat16)
    weight_in = expert_in[0]
    weight_out = expert_out[0]
    pre_active = jnp.dot(expert_rows, weight_in, preferred_element_type=jnp.float32)
    hidden_float, gelu_back = jax.vjp(gelu_curve, pre_active)
    hidden_units = hidden_float.astype(jnp.bfloat16)
    partial_rows = jnp.dot(hidden_units, weight_out, preferred_element_type=jnp.float32)
    grad_hidden = rows_dot(grad_rows, weight_out)
    grad_pre = gelu_back(grad_hidden)[0].astype(jnp.bfloat16)
    grad_inputs = rows_dot(grad_pre, weight_in)
    blocks = (tensor_size, experts_total, part, model_width)
    returned = combine(
        partial_rows.astype(jnp.bfloat16).reshape(blocks),
        grad_inputs.astype(jnp.bfloat16).reshape(blocks),
        2,
    ).reshape(2, tensor_size * part_rows, model_width)
    grad_expert_out = columns_dot(hidden_units, grad_rows)[None]
    grad_expert_in = columns_dot(expert_rows, grad_pre)[None]
    picked = jnp.dot(take_pick, returned[0], preferred_element_type=jnp.float32)
    grad_from_experts = jnp.dot(take_pick, returned[1], preferred_element_type=jnp.float32)
    layer_output = (after_attention + gate_value[:, None] * picked).astype(jnp.bfloat16)
    upstream = cotangent.astype(jnp.float32)
    grad_gate = jnp.sum(upstream * picked, axis=1)
    grad_logits = router_probs * (
        jnp.where(chosen, grad_gate[:, None], 0.0) - (gate_value * grad_gate)[:, None]
    )
    grad_router = jnp.dot(normed_wide.T, grad_logits, precision=largest_logit)
    grad_normed_second = grad_from_experts + jnp.dot(
        grad_logits, router_float.T, precision=largest_logit
    )
    grad_after, grad_gain_second = second_back(grad_normed_second)
    grad_residual = upstream + grad_after
    grad_attention_low = grad_residual.astype(jnp.bfloat16)
    grad_attention_out = columns_dot(mixed_heads, grad_attention_low)
    grad_mixed = rows_dot(grad_attention_low, attention_out).astype(jnp.bfloat16)
    grad_projected, offset_sums = local_call(
        functools.partial(attention_back_kernel, heads_here, score_scale),
        (
            jax.ShapeDtypeStruct((3, row_count, width_here), jnp.bfloat16),
            jax.ShapeDtypeStruct((heads_here, 2 * row_count), jnp.float32),
        ),
        shared_args + (log_total, grad_mixed),
    )
    grad_position_table = jnp.einsum(
        "hm,bm->bh", offset_sums, bucket_pick, precision=largest_logit
    )
    grad_projections = jnp.einsum(
        "cnh,nd->chd", grad_projected, normed_first, preferred_element_type=jnp.float32
    ).reshape(3 * width_here, model_width)
    first_scale = lax.rsqrt(
        jnp.mean(token_float * token_float, axis=-1, keepdims=True) + tiny_eps
    )
    table_row = jnp.pad(
        grad_position_table.reshape(1, -1),
        ((0, 0), (0, model_width - buckets_total * heads_here)),
    )
    small = jnp.concatenate([grad_gain_second[None], table_row, grad_router.T], axis=0)
    small = jnp.pad(small, ((0, 1 + (-small.shape[0] - 1) % 16), (0, 0)))
    grad_normed_first, large, small, grad_gain_first = finish(
        jnp.einsum("cnh,cdh->nd", grad_projected, projections, preferred_element_type=jnp.float32),
        token_float * first_scale,
        jnp.concatenate([grad_projections, grad_attention_out], axis=0),
        small,
        3,
    )
    grad_first_in = first_back(grad_normed_first)[0]
    grad_tokens = grad_residual + grad_first_in
    return (
        layer_output,
        grad_tokens,
        grad_gain_first,
        large[: 3 * width_here].reshape(3, width_here, model_width).transpose(0, 2, 1),
        large[3 * width_here :],
        small[1, : buckets_total * heads_here].reshape(buckets_total, heads_here),
        small[0],
        small[2 : 2 + experts_total].T,
        grad_expert_in,
        grad_expert_out,
    )


def solution(mesh):
    placed = (
        P("expert", None),
        P("expert", None),
        P("expert", None),
        P(),
        P(None, None, "tensor"),
        P("tensor", None),
        P(None, "tensor"),
        P(),
        P(),
        P("expert", None, "tensor"),
        P("expert", "tensor", None),
        P("expert", None),
    )
    return jax.shard_map(
        on_device,
        mesh=mesh,
        in_specs=placed,
        out_specs=(
            P("expert", None),
            P("expert", None),
            P(),
            P(None, None, "tensor"),
            P("tensor", None),
            P(None, "tensor"),
            P(),
            P(),
            P("expert", None, "tensor"),
            P("expert", "tensor", None),
        ),
        check_vma=False,
    )
```

```python
import functools

import jax
import jax.numpy as jnp
from jax import lax
from jax.experimental import pallas as pl
from jax.experimental.pallas import tpu as pltpu
from jax.sharding import PartitionSpec as P

edge_list = (1, 2, 3, 4, 5, 6, 7, 8, 12, 16, 23, 32, 46, 64, 91)
tiny_eps = 1e-06
masked_score = -1e30
sum_chunks = 4
largest_logit = lax.Precision.HIGHEST


def offset_buckets(row_count):
    span = 2 * row_count
    places = jnp.arange(span, dtype=jnp.int32)
    offsets = jnp.where(places < row_count, -places, span - places)
    bounds = jnp.asarray(edge_list, dtype=jnp.int32)
    passed = jnp.sum((jnp.abs(offsets)[:, None] >= bounds[None, :]).astype(jnp.int32), axis=1)
    return passed + 16 * (offsets < 0).astype(jnp.int32)


def document_ids(lengths_row, row_count):
    places = jnp.arange(row_count, dtype=jnp.int32)
    endings = jnp.cumsum(lengths_row)
    return jnp.sum((places[:, None] >= endings[None, :]).astype(jnp.int32), axis=1)


def rms_scale(values, gain):
    return values * lax.rsqrt(jnp.mean(values * values, axis=-1, keepdims=True) + tiny_eps) * gain


def gelu_curve(values):
    return (
        0.5
        * values
        * (1.0 + jnp.tanh(0.7978845608 * (values + 0.044715 * values * values * values)))
    )


def softmax_rows(scores):
    top_score = jnp.max(scores, axis=-1, keepdims=True)
    raised = jnp.exp(scores - top_score)
    return raised / jnp.sum(raised, axis=-1, keepdims=True)


MESH = pl.DeviceIdType.MESH


def vmem():
    return pl.BlockSpec(memory_space=pltpu.VMEM)


def tensor_places():
    mine = lax.axis_index("tensor")
    core = mine % 2
    side = mine // 2
    return mine, core, side, side * 2 + (1 - core), (1 - side) * 2 + core


def greet(devices):
    barrier = pltpu.get_barrier_semaphore()
    for device in devices:
        pl.semaphore_signal(barrier, inc=1, device_id=device, device_id_type=MESH)
    pl.semaphore_wait(barrier, len(devices))


def remote(source, target, send_sem, recv_sem, device):
    return pltpu.make_async_remote_copy(
        src_ref=source,
        dst_ref=target,
        send_sem=send_sem,
        recv_sem=recv_sem,
        device_id=device,
        device_id_type=MESH,
    )


def tensor_sum_steps(x_ref, o_ref, near, chip, far, send_sem, recv_sem):
    _, core, _, sibling, across = tensor_places()
    half = x_ref.shape[0] // 2
    chunk = half // sum_chunks
    copies = []

    def rows_of(which, turn):
        return pl.ds(pl.multiple_of(which * half + turn * chunk, chunk), chunk)

    def begin(source, target, place, device):
        copy = remote(source, target, send_sem.at[place], recv_sem.at[place], {"tensor": device})
        copy.start()
        copies.append(copy)
        return copy

    first = [
        begin(x_ref.at[rows_of(1 - core, turn)], near.at[turn], turn, sibling)
        for turn in range(sum_chunks)
    ]
    yield
    second = []
    for turn in range(sum_chunks):
        first[turn].wait_recv()
        own = x_ref[rows_of(core, turn)].astype(jnp.float32)
        chip[turn] = (own + near[turn].astype(jnp.float32)).astype(chip.dtype)
        second.append(begin(chip.at[turn], far.at[turn], sum_chunks + turn, across))
    yield
    third = []
    for turn in range(sum_chunks):
        second[turn].wait_recv()
        own = rows_of(core, turn)
        o_ref[own] = chip[turn].astype(jnp.float32) + far[turn].astype(jnp.float32)
        third.append(begin(o_ref.at[own], o_ref.at[own], 2 * sum_chunks + turn, sibling))
    yield
    for copy in third:
        copy.wait_recv()
    for copy in copies:
        copy.wait_send()
    yield


def tensor_sum_scratch(rows, width):
    chunk = pltpu.VMEM((sum_chunks, rows // 2 // sum_chunks, width), jnp.bfloat16)
    sems = pltpu.SemaphoreType.DMA((3 * sum_chunks,))
    return [chunk, chunk, chunk, sems, sems]


def tensor_sum_kernel(*refs):
    _, _, _, sibling, across = tensor_places()
    greet([{"tensor": sibling}, {"tensor": across}])
    for _ in tensor_sum_steps(*refs):
        pass


def tensor_total(value, collective_id):
    rows, width = value.shape
    if lax.axis_size("tensor") != 4 or rows % (32 * sum_chunks):
        return lax.psum(value, "tensor")
    return pl.pallas_call(
        tensor_sum_kernel,
        out_shape=jax.ShapeDtypeStruct((rows, width), jnp.float32),
        in_specs=[vmem()],
        out_specs=vmem(),
        scratch_shapes=tensor_sum_scratch(rows, width),
        compiler_params=pltpu.CompilerParams(
            collective_id=collective_id, has_side_effects=True, vmem_limit_bytes=32 * 2**20
        ),
        cost_estimate=pl.CostEstimate(flops=0, bytes_accessed=30_000_000, transcendentals=0),
    )(value.astype(jnp.bfloat16))


def share_over_tensor(places, pieces, sems):
    mine, _, _, sibling, across = places
    across_send, across_recv, near_send, near_recv, pass_send, pass_recv = sems

    def begin(step):
        far = remote(
            pieces(mine, step),
            pieces(mine, step),
            across_send.at[step],
            across_recv.at[step],
            {"tensor": across},
        )
        close = remote(
            pieces(mine, step),
            pieces(mine, step),
            near_send.at[step],
            near_recv.at[step],
            {"tensor": sibling},
        )
        far.start()
        close.start()
        return far, close

    def forward(step):
        onward = remote(
            pieces(across, step),
            pieces(across, step),
            pass_send.at[step],
            pass_recv.at[step],
            {"tensor": sibling},
        )
        onward.start()
        return onward

    return begin, forward


def dispatch_kernel(groups, send_ref, o_ref, out_send, out_recv, *sems):
    here = lax.axis_index("expert")
    places = tensor_places()
    mine, _, _, sibling, across = places
    peers = [lax.rem(here + step, groups) for step in range(groups)]
    greet([{"expert": peer} for peer in peers[1:]] + [{"tensor": sibling}, {"tensor": across}])
    copies = [None]
    for step in range(1, groups):
        copy = remote(
            send_ref.at[peers[step]],
            o_ref.at[mine, here],
            out_send.at[step],
            out_recv.at[step],
            {"expert": peers[step]},
        )
        copy.start()
        copies.append(copy)
    o_ref[mine, here] = send_ref[here]

    def pieces(quarter, step):
        return o_ref.at[quarter, lax.rem(here + groups - step, groups)]

    begin, forward = share_over_tensor(places, pieces, sems)
    shared = []
    for step in range(groups):
        if step:
            copies[step].wait_recv()
        shared.append(begin(step))
    onward = []
    for step in range(groups):
        shared[step][0].wait_recv()
        onward.append(forward(step))
    for step in range(groups):
        if step:
            copies[step].wait_send()
        shared[step][0].wait_send()
        shared[step][1].wait()
        onward[step].wait()


def kernels_fit(part_rows):
    return lax.axis_size("tensor") == 4 and lax.axis_size("expert") <= 8 and part_rows % 16 == 0


def dispatch(send, collective_id):
    groups, part, width = send.shape
    if not kernels_fit(part):
        received = lax.all_to_all(send, "expert", split_axis=0, concat_axis=0, tiled=True)
        return lax.all_gather(received, "tensor", axis=0, tiled=False)
    sems = pltpu.SemaphoreType.DMA((groups,))
    return pl.pallas_call(
        functools.partial(dispatch_kernel, groups),
        out_shape=jax.ShapeDtypeStruct((lax.axis_size("tensor"),) + send.shape, send.dtype),
        in_specs=[vmem()],
        out_specs=vmem(),
        scratch_shapes=[sems] * 8,
        compiler_params=pltpu.CompilerParams(
            collective_id=collective_id, has_side_effects=True, vmem_limit_bytes=32 * 2**20
        ),
        cost_estimate=pl.CostEstimate(flops=0, bytes_accessed=50_000_000, transcendentals=0),
    )(send)


def combine_kernel(groups, ahead_ref, back_ref, o_ref, near, chip, far, total, *sems):
    near_send, near_recv, far_send, far_recv, out_send, out_recv = sems[:6]
    here = lax.axis_index("expert")
    places = tensor_places()
    mine, core, side, sibling, across = places
    peers = [lax.rem(here + step, groups) for step in range(groups)]
    greet([{"expert": peer} for peer in peers[1:]] + [{"tensor": sibling}, {"tensor": across}])
    inputs = (ahead_ref, back_ref)
    sides = (1 - side, side)
    gather = []
    for kind in range(2):
        for turn in range(2):
            copy = remote(
                inputs[kind].at[sides[turn] * 2 + (1 - core)],
                near.at[2 * kind + turn],
                near_send.at[2 * kind + turn],
                near_recv.at[2 * kind + turn],
                {"tensor": sibling},
            )
            copy.start()
            gather.append(copy)
    crossing = []
    for kind in range(2):
        for turn in range(2):
            gather[2 * kind + turn].wait_recv()
            chip[2 * kind + turn] = (
                inputs[kind][sides[turn] * 2 + core].astype(jnp.float32)
                + near[2 * kind + turn].astype(jnp.float32)
            ).astype(chip.dtype)
            if turn == 0:
                copy = remote(
                    chip.at[2 * kind],
                    far.at[kind],
                    far_send.at[kind],
                    far_recv.at[kind],
                    {"tensor": across},
                )
                copy.start()
                crossing.append(copy)
    outgoing = []
    for kind in range(2):
        crossing[kind].wait_recv()
        total[kind] = (
            chip[2 * kind + 1].astype(jnp.float32) + far[kind].astype(jnp.float32)
        ).astype(total.dtype)
        outgoing.append(None)
        for step in range(1, groups):
            copy = remote(
                total.at[kind, peers[step]],
                o_ref.at[kind, mine, here],
                out_send.at[kind * groups + step],
                out_recv.at[kind * groups + step],
                {"expert": peers[step]},
            )
            copy.start()
            outgoing.append(copy)
        o_ref[kind, mine, here] = total[kind, here]

    def pieces(quarter, place):
        return o_ref.at[place // groups, quarter, lax.rem(here + groups - place % groups, groups)]

    begin, forward = share_over_tensor(places, pieces, sems[6:])
    shared = []
    onward = []
    for place in range(2 * groups):
        if place % groups:
            outgoing[place].wait_recv()
        shared.append(begin(place))
        if place >= groups:
            shared[place - groups][0].wait_recv()
            onward.append(forward(place - groups))
    for place in range(groups, 2 * groups):
        shared[place][0].wait_recv()
        onward.append(forward(place))
    for copy in gather + crossing:
        copy.wait_send()
    for place in range(2 * groups):
        if place % groups:
            outgoing[place].wait_send()
        shared[place][0].wait_send()
        shared[place][1].wait()
        onward[place].wait()


def combine(ahead, back, collective_id):
    quarters, groups, part, width = ahead.shape
    if not kernels_fit(part):
        both = jnp.stack([ahead, back], axis=1).astype(jnp.float32)
        mine = lax.psum_scatter(both, "tensor", scatter_dimension=0, tiled=False)
        received = lax.all_to_all(
            mine.astype(jnp.bfloat16), "expert", split_axis=1, concat_axis=1, tiled=True
        )
        return lax.all_gather(received, "tensor", axis=1, tiled=False)
    piece = (groups, part, width)
    one = pltpu.SemaphoreType.DMA((2 * groups,))
    return pl.pallas_call(
        functools.partial(combine_kernel, groups),
        out_shape=jax.ShapeDtypeStruct((2,) + ahead.shape, jnp.bfloat16),
        in_specs=[vmem(), vmem()],
        out_specs=vmem(),
        scratch_shapes=[
            pltpu.VMEM((4,) + piece, jnp.bfloat16),
            pltpu.VMEM((4,) + piece, jnp.bfloat16),
            pltpu.VMEM((2,) + piece, jnp.bfloat16),
            pltpu.VMEM((2,) + piece, jnp.bfloat16),
            pltpu.SemaphoreType.DMA((4,)),
            pltpu.SemaphoreType.DMA((4,)),
            pltpu.SemaphoreType.DMA((2,)),
            pltpu.SemaphoreType.DMA((2,)),
        ]
        + [one] * 8,
        compiler_params=pltpu.CompilerParams(
            collective_id=collective_id, has_side_effects=True, vmem_limit_bytes=40 * 2**20
        ),
        cost_estimate=pl.CostEstimate(flops=0, bytes_accessed=120_000_000, transcendentals=0),
    )(ahead, back)


def finish_kernel(
    groups, x_ref, unit_ref, big_ref, small_ref, o_ref, big_out, small_out, *scratch
):
    (
        pair_buf,
        line_send,
        line_buf,
        small_send,
        small_pair,
        small_buf,
        pair_sems,
        line_sems,
        spread_sems,
        pass_sems,
        small_sems,
    ) = scratch[:11]
    here = lax.axis_index("expert")
    _, _, _, sibling, across = tensor_places()
    lines = groups // 2
    place = here // 2
    lane = here % 2
    pair = place * 2 + (1 - lane)
    places = [lax.rem(place + step, lines) for step in range(lines)]
    friends = [pair] + [places[step] * 2 + lane for step in range(1, lines)]
    greet([{"expert": friend} for friend in friends] + [{"tensor": sibling}, {"tensor": across}])
    copies = []

    def begin(source, target, sems, index, device):
        copy = remote(source, target, sems.at[0, index], sems.at[1, index], {"expert": device})
        copy.start()
        copies.append(copy)
        return copy

    order = list(range(1, lines)) + [0]
    pairs = {}
    for step in order:
        pairs[step] = begin(
            big_ref.at[places[step] * 2 + (1 - lane)], pair_buf.at[step], pair_sems, step, pair
        )
    steps = tensor_sum_steps(x_ref, o_ref, *scratch[11:])
    next(steps)
    next(steps)
    along = {}
    for step in order:
        pairs[step].wait_recv()
        line_send[step] = (
            big_ref[places[step] * 2 + lane].astype(jnp.float32)
            + pair_buf[step].astype(jnp.float32)
        ).astype(line_send.dtype)
        if step:
            along[step] = begin(
                line_send.at[step], line_buf.at[step], line_sems, step, places[step] * 2 + lane
            )
    next(steps)
    next(steps)
    gain = jnp.sum(o_ref[...] * unit_ref[...], axis=0, keepdims=True)
    last = lax.broadcasted_iota(jnp.int32, small_ref.shape, 0) == small_ref.shape[0] - 1
    small_send[0] = jnp.where(last, gain, small_ref[...])
    small_first = begin(small_send.at[0], small_pair, small_sems, 0, pair)
    total = line_send[0].astype(jnp.float32)
    for step in range(1, lines):
        along[step].wait_recv()
        total = total + line_buf[step].astype(jnp.float32)
    big_out[here] = total.astype(big_out.dtype)
    spread = {}
    for step in order:
        device = places[step] * 2 + lane if step else pair
        spread[step] = begin(big_out.at[here], big_out.at[here], spread_sems, step, device)
    small_first.wait_recv()
    small_send[1] = small_send[0] + small_pair[...]
    small_buf[place] = small_send[1]
    smalls = [
        begin(small_send.at[1], small_buf.at[place], small_sems, step, friends[step])
        for step in range(1, lines)
    ]
    passed = []
    for step in range(1, lines):
        spread[step].wait_recv()
        came = lax.rem(place + lines - step, lines) * 2 + lane
        passed.append(begin(big_out.at[came], big_out.at[came], pass_sems, step, pair))
    for copy in smalls + [spread[0]] + passed:
        copy.wait_recv()
    for copy in copies:
        copy.wait_send()
    small_sum = small_buf[0]
    for source in range(1, lines):
        small_sum = small_sum + small_buf[source]
    small_out[...] = small_sum


def finish(partial, unit, large, small, collective_id):
    rows, width = partial.shape
    groups = lax.axis_size("expert")
    if (
        lax.axis_size("tensor") != 4
        or groups != 8
        or large.shape[0] % (16 * groups)
        or rows % (32 * sum_chunks)
    ):
        total = lax.psum(partial, "tensor")
        gain, small = lax.psum((jnp.sum(total * unit, axis=0), small), "expert")
        large = lax.psum(large.astype(jnp.bfloat16), "expert")
        return total, large.astype(jnp.float32), small, gain
    piece = (large.shape[0] // groups, width)
    lines = groups // 2
    few = pltpu.SemaphoreType.DMA((2, lines))
    total, large, small = pl.pallas_call(
        functools.partial(finish_kernel, groups),
        out_shape=(
            jax.ShapeDtypeStruct((rows, width), jnp.float32),
            jax.ShapeDtypeStruct((groups,) + piece, jnp.bfloat16),
            jax.ShapeDtypeStruct(small.shape, jnp.float32),
        ),
        in_specs=[vmem()] * 4,
        out_specs=(vmem(),) * 3,
        scratch_shapes=[
            pltpu.VMEM((lines,) + piece, jnp.bfloat16),
            pltpu.VMEM((lines,) + piece, jnp.bfloat16),
            pltpu.VMEM((lines,) + piece, jnp.bfloat16),
            pltpu.VMEM((2,) + small.shape, jnp.float32),
            pltpu.VMEM(small.shape, jnp.float32),
            pltpu.VMEM((lines,) + small.shape, jnp.float32),
            few,
            few,
            few,
            few,
            few,
        ]
        + tensor_sum_scratch(rows, width),
        compiler_params=pltpu.CompilerParams(
            collective_id=collective_id, has_side_effects=True, vmem_limit_bytes=40 * 2**20
        ),
        cost_estimate=pl.CostEstimate(flops=0, bytes_accessed=100_000_000, transcendentals=0),
    )(partial.astype(jnp.bfloat16), unit, large.astype(jnp.bfloat16).reshape((groups,) + piece), small)
    return total, large.astype(jnp.float32).reshape(-1, width), small, small[-1]


def rows_dot(left, right):
    return lax.dot_general(
        left, right, (((1,), (1,)), ((), ())), preferred_element_type=jnp.float32
    )


def columns_dot(left, right):
    return lax.dot_general(
        left, right, (((0,), (0,)), ((), ())), preferred_element_type=jnp.float32
    )


def masked_scores(queries, keys_here, line, doc_column, doc_row, score_scale):
    row_count = queries.shape[0]
    bias = line
    while bias.shape[0] < row_count:
        bias = jnp.concatenate([bias, pltpu.roll(bias, bias.shape[0], 1)], axis=0)
    raw = rows_dot(queries, keys_here) * score_scale + bias[:, :row_count]
    return jnp.where(doc_column == doc_row, raw, masked_score)


def attention_kernel(heads, scale, qkv_ref, line_ref, column_ref, row_ref, mixed_ref, log_ref):
    size = qkv_ref.shape[2] // heads
    for head in range(heads):
        part = slice(head * size, head * size + size)
        scores = masked_scores(
            qkv_ref[0, :, part],
            qkv_ref[1, :, part],
            line_ref[head : head + 1, :],
            column_ref[...],
            row_ref[...],
            scale,
        )
        top_score = jnp.max(scores, axis=-1, keepdims=True)
        raised = jnp.exp(scores - top_score)
        totals = jnp.sum(raised, axis=-1, keepdims=True)
        soft = (raised / totals).astype(jnp.bfloat16)
        mixed_ref[:, part] = jnp.dot(
            soft, qkv_ref[2, :, part], preferred_element_type=jnp.float32
        ).astype(mixed_ref.dtype)
        log_ref[head] = top_score + jnp.log(totals)


def attention_back_kernel(
    heads, scale, qkv_ref, line_ref, column_ref, row_ref, log_ref, up_ref, grad_ref, sums_ref
):
    size = qkv_ref.shape[2] // heads
    row_count = qkv_ref.shape[1]
    for head in range(heads):
        part = slice(head * size, head * size + size)
        queries = qkv_ref[0, :, part]
        keys_here = qkv_ref[1, :, part]
        upstream = up_ref[:, part]
        scores = masked_scores(
            queries,
            keys_here,
            line_ref[head : head + 1, :],
            column_ref[...],
            row_ref[...],
            scale,
        )
        soft = jnp.exp(scores - log_ref[head])
        grad_soft = rows_dot(upstream, qkv_ref[2, :, part])
        centre = jnp.sum(soft * grad_soft, axis=-1, keepdims=True)
        grad_scores = (soft * (grad_soft - centre)).astype(jnp.bfloat16)
        grad_ref[2, :, part] = columns_dot(soft.astype(jnp.bfloat16), upstream).astype(
            grad_ref.dtype
        )
        grad_ref[0, :, part] = (
            jnp.dot(grad_scores, keys_here, preferred_element_type=jnp.float32) * scale
        ).astype(grad_ref.dtype)
        grad_ref[1, :, part] = (columns_dot(grad_scores, queries) * scale).astype(grad_ref.dtype)
        wide = grad_scores.astype(jnp.float32)
        wide = jnp.concatenate([wide, jnp.zeros_like(wide)], axis=1)
        while wide.shape[0] > 1:
            half = wide.shape[0] // 2
            wide = wide[:half] + pltpu.roll(wide[half:], 2 * row_count - half, 1)
        sums_ref[head : head + 1, :] = wide


def local_call(kernel, outs, args):
    return pl.pallas_call(
        kernel,
        out_shape=outs,
        in_specs=[vmem()] * len(args),
        out_specs=tuple(vmem() for _ in outs),
        compiler_params=pltpu.CompilerParams(vmem_limit_bytes=40 * 2**20),
        cost_estimate=pl.CostEstimate(
            flops=1_000_000_000, bytes_accessed=30_000_000, transcendentals=1_000_000
        ),
    )(*args)


def on_device(
    tokens,
    doc_lengths,
    routes,
    gain_first,
    projections,
    attention_out,
    relative_bias_table,
    gain_second,
    router_weight,
    expert_in,
    expert_out,
    cotangent,
):
    row_count = tokens.shape[0]
    model_width = tokens.shape[1]
    heads_here = relative_bias_table.shape[1]
    buckets_total = relative_bias_table.shape[0]
    width_here = projections.shape[2]
    head_size = width_here // heads_here
    experts_total = router_weight.shape[1]
    tensor_size = lax.axis_size("tensor")
    capacity = max(2, 2 * row_count // experts_total)
    part = capacity // tensor_size
    part_rows = experts_total * part
    score_scale = head_size ** (-0.5)
    quarter = lax.axis_index("tensor")

    route_column = routes[:, 0]
    chosen = route_column[:, None] == jnp.arange(experts_total, dtype=jnp.int32)[None, :]
    earlier = jnp.cumsum(chosen.astype(jnp.int32), axis=0) - 1
    slot = jnp.sum(jnp.where(chosen, earlier, 0), axis=1)
    place = (slot // part) * part_rows + route_column * part + slot % part
    own_place = place - quarter * part_rows
    send_pick = (
        jnp.arange(part_rows, dtype=jnp.int32)[:, None] == own_place[None, :]
    ).astype(jnp.bfloat16)
    take_pick = (
        place[:, None] == jnp.arange(tensor_size * part_rows, dtype=jnp.int32)[None, :]
    ).astype(jnp.bfloat16)

    def placed_rows(rows):
        picked_rows = jnp.dot(send_pick, rows, preferred_element_type=jnp.float32)
        return picked_rows.astype(jnp.bfloat16).reshape(experts_total, part, rows.shape[1])

    slot_pick = (
        jnp.arange(experts_total * capacity, dtype=jnp.int32)[:, None]
        == (route_column * capacity + slot)[None, :]
    ).astype(jnp.bfloat16)
    upstream_slots = (
        jnp.dot(slot_pick, cotangent, preferred_element_type=jnp.float32)
        .astype(jnp.bfloat16)
        .reshape(experts_total, capacity, model_width)
    )
    upstream_rows = (
        lax.all_to_all(upstream_slots, "expert", split_axis=0, concat_axis=0, tiled=True)
        .reshape(experts_total, tensor_size, part, model_width)
        .transpose(1, 0, 2, 3)
    )

    token_float = tokens.astype(jnp.float32)
    normed_float, first_back = jax.vjp(rms_scale, token_float, gain_first)
    normed_first = normed_float.astype(jnp.bfloat16)
    projected = jnp.einsum(
        "nd,cdh->cnh", normed_first, projections, preferred_element_type=jnp.float32
    ).astype(jnp.bfloat16)
    bucket_pick = (
        jnp.arange(buckets_total, dtype=jnp.int32)[:, None] == offset_buckets(row_count)[None, :]
    ).astype(jnp.float32)
    bias_line = jnp.einsum("bh,bm->hm", relative_bias_table, bucket_pick, precision=largest_logit)
    documents = document_ids(doc_lengths[0], row_count)
    shared_args = (projected, bias_line, documents[:, None], documents[None, :])
    mixed_heads, log_total = local_call(
        functools.partial(attention_kernel, heads_here, score_scale),
        (
            jax.ShapeDtypeStruct((row_count, width_here), jnp.bfloat16),
            jax.ShapeDtypeStruct((heads_here, row_count, 1), jnp.float32),
        ),
        shared_args,
    )
    after_attention = token_float + tensor_total(
        jnp.dot(mixed_heads, attention_out, preferred_element_type=jnp.float32), 0
    )
    second_float, second_back = jax.vjp(rms_scale, after_attention, gain_second)
    normed_second = second_float.astype(jnp.bfloat16)
    normed_wide = normed_second.astype(jnp.float32)
    router_float = router_weight.astype(jnp.float32)
    router_probs = softmax_rows(jnp.dot(normed_wide, router_float, precision=largest_logit))
    gate_value = jnp.sum(jnp.where(chosen, router_probs, 0.0), axis=1)

    gate_high = lax.reduce_precision(gate_value, 8, 7)
    gate_rest = gate_value - gate_high
    gate_middle = lax.reduce_precision(gate_rest, 8, 7)
    gate_terms = jnp.stack([gate_high, gate_middle, gate_rest - gate_middle], axis=1)
    gate_columns = jnp.pad(gate_terms.astype(jnp.bfloat16), ((0, 0), (0, 125)))
    arrived = dispatch(placed_rows(jnp.concatenate([normed_second, gate_columns], axis=1)), 1)
    arrived = arrived.reshape(tensor_size * part_rows, model_width + 128)
    expert_rows = arrived[:, :model_width]
    row_gates = jnp.sum(
        arrived[:, model_width : model_width + 3].astype(jnp.float32), axis=1, keepdims=True
    )
    grad_rows = (
        row_gates * upstream_rows.reshape(expert_rows.shape).astype(jnp.float32)
    ).astype(jnp.bfloat16)
    weight_in = expert_in[0]
    weight_out = expert_out[0]
    pre_active = jnp.dot(expert_rows, weight_in, preferred_element_type=jnp.float32)
    hidden_float, gelu_back = jax.vjp(gelu_curve, pre_active)
    hidden_units = hidden_float.astype(jnp.bfloat16)
    partial_rows = jnp.dot(hidden_units, weight_out, preferred_element_type=jnp.float32)
    grad_hidden = rows_dot(grad_rows, weight_out)
    grad_pre = gelu_back(grad_hidden)[0].astype(jnp.bfloat16)
    grad_inputs = rows_dot(grad_pre, weight_in)
    blocks = (tensor_size, experts_total, part, model_width)
    returned = combine(
        partial_rows.astype(jnp.bfloat16).reshape(blocks),
        grad_inputs.astype(jnp.bfloat16).reshape(blocks),
        2,
    ).reshape(2, tensor_size * part_rows, model_width)
    grad_expert_out = columns_dot(hidden_units, grad_rows)[None]
    grad_expert_in = columns_dot(expert_rows, grad_pre)[None]
    picked = jnp.dot(take_pick, returned[0], preferred_element_type=jnp.float32)
    grad_from_experts = jnp.dot(take_pick, returned[1], preferred_element_type=jnp.float32)
    layer_output = (after_attention + gate_value[:, None] * picked).astype(jnp.bfloat16)
    upstream = cotangent.astype(jnp.float32)
    grad_gate = jnp.sum(upstream * picked, axis=1)
    grad_logits = router_probs * (
        jnp.where(chosen, grad_gate[:, None], 0.0) - (gate_value * grad_gate)[:, None]
    )
    grad_router = jnp.dot(normed_wide.T, grad_logits, precision=largest_logit)
    grad_normed_second = grad_from_experts + jnp.dot(
        grad_logits, router_float.T, precision=largest_logit
    )
    grad_after, grad_gain_second = second_back(grad_normed_second)
    grad_residual = upstream + grad_after
    grad_attention_low = grad_residual.astype(jnp.bfloat16)
    grad_attention_out = columns_dot(mixed_heads, grad_attention_low)
    grad_mixed = rows_dot(grad_attention_low, attention_out).astype(jnp.bfloat16)
    grad_projected, offset_sums = local_call(
        functools.partial(attention_back_kernel, heads_here, score_scale),
        (
            jax.ShapeDtypeStruct((3, row_count, width_here), jnp.bfloat16),
            jax.ShapeDtypeStruct((heads_here, 2 * row_count), jnp.float32),
        ),
        shared_args + (log_total, grad_mixed),
    )
    grad_position_table = jnp.einsum(
        "hm,bm->bh", offset_sums, bucket_pick, precision=largest_logit
    )
    grad_projections = jnp.einsum(
        "cnh,nd->chd", grad_projected, normed_first, preferred_element_type=jnp.float32
    ).reshape(3 * width_here, model_width)
    first_scale = lax.rsqrt(
        jnp.mean(token_float * token_float, axis=-1, keepdims=True) + tiny_eps
    )
    table_row = jnp.pad(
        grad_position_table.reshape(1, -1),
        ((0, 0), (0, model_width - buckets_total * heads_here)),
    )
    small = jnp.concatenate([grad_gain_second[None], table_row, grad_router.T], axis=0)
    small = jnp.pad(small, ((0, 1 + (-small.shape[0] - 1) % 16), (0, 0)))
    grad_normed_first, large, small, grad_gain_first = finish(
        jnp.einsum("cnh,cdh->nd", grad_projected, projections, preferred_element_type=jnp.float32),
        token_float * first_scale,
        jnp.concatenate([grad_projections, grad_attention_out], axis=0),
        small,
        3,
    )
    grad_first_in = first_back(grad_normed_first)[0]
    grad_tokens = grad_residual + grad_first_in
    return (
        layer_output,
        grad_tokens,
        grad_gain_first,
        large[: 3 * width_here].reshape(3, width_here, model_width).transpose(0, 2, 1),
        large[3 * width_here :],
        small[1, : buckets_total * heads_here].reshape(buckets_total, heads_here),
        small[0],
        small[2 : 2 + experts_total].T,
        grad_expert_in,
        grad_expert_out,
    )


def solution(mesh):
    placed = (
        P("expert", None),
        P("expert", None),
        P("expert", None),
        P(),
        P(None, None, "tensor"),
        P("tensor", None),
        P(None, "tensor"),
        P(),
        P(),
        P("expert", None, "tensor"),
        P("expert", "tensor", None),
        P("expert", None),
    )
    return jax.shard_map(
        on_device,
        mesh=mesh,
        in_specs=placed,
        out_specs=(
            P("expert", None),
            P("expert", None),
            P(),
            P(None, None, "tensor"),
            P("tensor", None),
            P(None, "tensor"),
            P(),
            P(),
            P("expert", None, "tensor"),
            P("expert", "tensor", None),
        ),
        check_vma=False,
    )
```
